32 devices in a mesh: dom: 8 (over z, x), feat: 4 (over y, core).
Axes of the slice: x: 2, y: 2, z: 4, core: 2. Of those that a mesh axis runs over, the one named last changes fastest.
Arguments:
- inputs_t: bfloat16 [128, 32768], P('feat', 'dom'), may hold values from -6 to 6
- tiles_first: bfloat16 [512, 128, 128], P('dom'), may hold values from 9e-05 to 1, as said below
- first_dst: int32 [512], P('dom'), may hold values from 0 to 15, as said below
- first_src: int32 [512], P('dom'), may hold values from 0 to 31
- w1_self: bfloat16 [128, 256], P('feat'), may hold values from -0.5 to 0.5
- w1_neigh: bfloat16 [128, 256], P('feat'), may hold values from -6 to 6
- bias_first: float32 [256], replicated, may hold values from -3 to 3
- fetch_ids: int32 [32, 32, 2], P(None, ('dom', 'feat')), may hold values from 0 to 3, as said below
- tiles_out: bfloat16 [12288, 128, 128], P(('dom', 'feat')), may hold values from 9e-05 to 1, as said below
- out_dst: int32 [12288], P(('dom', 'feat')), may hold values from 0 to 3, as said below
- out_src: int32 [12288], P(('dom', 'feat')), may hold values from 0 to 63, as said below
- output_self_weight: bfloat16 [256, 172], replicated, may hold values from -1 to 1
- output_neighbour_weight: bfloat16 [256, 172], replicated, may hold values from -2 to 2
- bias_out: float32 [172], replicated, may hold values from -4 to 4
- labels: int32 [16384], P(('dom', 'feat')), may hold values from 0 to 171
Outputs:
- grad_w1_self: float32 [128, 256], P('feat')
- grad_w1_neigh: float32 [128, 256], P('feat')
- grad_b1: float32 [256], replicated
- grad_w3_self: float32 [256, 172], replicated
- grad_w3_neigh: float32 [256, 172], replicated
- grad_b3: float32 [172], replicated
The draws below stay inside these ranges and needn't reach their ends.
Inputs may be any that keep to these rules, and one draw needn't show every extreme that they name: `first_dst`: each partition's first-layer tiles name every destination block at least once. `fetch_ids`: the 2 blocks one device requests from one owner are different. `out_dst`: each device's tiles name every local target block at least once. `out_src`: each device's tiles read every one of its slots at least once. `tiles_first`: every entry is positive. `tiles_out`: every entry is positive.
All inputs are finite; a program needn't handle non-finite values.
Results may differ from the reference program's by a relative error of at most 0.0034.
The reference program's roundings to bfloat16 on the way count: a program that leaves them out, or rounds other values in their place, can miss the bound.
Values may be sent and summed in bfloat16 or wider, within the bound.
No kernel may reach another device: no remote copies, remote signals or barrier semaphores. Data moves between devices by JAX's collectives and lax.ppermute only.
A program may use at most 192 MiB of HBM per device.

```python
import math
import jax
import jax.numpy as jnp
import numpy as np
from jax import lax

FEATURES = 128
HIDDEN_WIDTH = 256
CLASSES = 172
TILE_ROWS = 128
BLOCKS_DEV = 4
SLOTS_PEER = 2
TILES_BLOCK = 96
FIRST_FAN = 4
INPUT_BLOCKS = 32
TILES_FIRST = 64
TILES_OUT = 384
INPUT_NODES = 32768
TARGETS = 16384
N_DOM = 8
N_FEAT = 4


def spread_cover(key, groups, length, cover):
    keys = jax.random.split(key, groups)

    def single(subkey):
        fill_key, order_key = jax.random.split(subkey)
        base = jnp.concatenate([jnp.arange(cover, dtype=jnp.int32), jax.random.randint(fill_key, (length - cover,), 0, cover, dtype=jnp.int32)])
        return base[jax.random.permutation(order_key, length)]
    return jax.vmap(single)(keys).reshape(-1)


def draw_tiles_first(key, part):
    key = jax.random.fold_in(key, 13)
    chance = 12.0 / (FIRST_FAN * TILE_ROWS)
    grid = jax.random.uniform(key, (N_DOM * TILES_FIRST, TILE_ROWS, TILE_ROWS), jnp.float32)
    share = jnp.minimum(grid / chance, 1.0)
    rest = jnp.maximum(grid - chance, 0.0) / (1.0 - chance)
    spike = 0.1 * jnp.exp(2.302585 * share)
    return jnp.where(grid < chance, spike, 0.0001 * (1.0 + rest)).astype(jnp.bfloat16)


def draw_first_dst(key, part):
    key = jax.random.fold_in(key, 3)
    return spread_cover(key, N_DOM, TILES_FIRST, N_FEAT * BLOCKS_DEV)


def draw_fetch_ids(key, part):
    key = jax.random.fold_in(key, 5)
    first_key, second_key = jax.random.split(key)
    devices = N_DOM * N_FEAT
    first = jax.random.randint(first_key, (devices, devices, 1), 0, BLOCKS_DEV, dtype=jnp.int32)
    offset = jax.random.randint(second_key, (devices, devices, 1), 1, BLOCKS_DEV, dtype=jnp.int32)
    return jnp.concatenate([first, (first + offset) % BLOCKS_DEV], axis=2)


def draw_tiles_out(key, part):
    key = jax.random.fold_in(key, 17)
    chance = 12.0 / (TILES_BLOCK * TILE_ROWS)
    grid = jax.random.uniform(key, (N_DOM * N_FEAT * TILES_OUT, TILE_ROWS, TILE_ROWS), jnp.float32)
    share = jnp.minimum(grid / chance, 1.0)
    rest = jnp.maximum(grid - chance, 0.0) / (1.0 - chance)
    background = 9e-05 * jnp.exp(4.710531 * rest)
    spike = 0.1 * jnp.exp(2.302585 * share)
    return jnp.where(grid < chance, spike, background).astype(jnp.bfloat16)


def draw_out_dst(key, part):
    key = jax.random.fold_in(key, 7)
    return spread_cover(key, N_DOM * N_FEAT, TILES_OUT, BLOCKS_DEV)


def draw_out_src(key, part):
    key = jax.random.fold_in(key, 11)
    return spread_cover(key, N_DOM * N_FEAT, TILES_OUT, N_DOM * N_FEAT * SLOTS_PEER)


def touch_ends(result, stream_key, smallest, top_value):
    spot = [jax.random.randint(jax.random.fold_in(stream_key, axis), (), 0, length) for axis, length in enumerate(result.shape)]
    widest = result.shape.index(max(result.shape))
    next_to = spot[:widest] + [(spot[widest] + 1) % result.shape[widest]] + spot[widest + 1:]
    return result.at[tuple(spot)].set(smallest).at[tuple(next_to)].set(top_value)


def steps_of(stream_key, extent, cuts, low, top_value):
    level, own = 1.0, jax.random.fold_in(stream_key, 6)
    for axis_at, blocks in cuts:
        heights = jnp.exp(jax.random.uniform(jax.random.fold_in(own, axis_at), (blocks,), jnp.float32, low / len(cuts), top_value / len(cuts)))
        level = level * jnp.repeat(heights, extent[axis_at] // blocks).reshape([-1 if axis == axis_at else 1 for axis in range(len(extent))])
    return level


def rank_bounds(count, skew):
    weights = [(1 << 20) // math.isqrt(grade ** skew) + 1 for grade in range(1, count + 1)]
    deviation = 1 + sum(weights) // (1 << 30)
    return np.cumsum(np.array([max(1, weight // deviation) for weight in weights]))


def ranked(key, dims, count, skew):
    listing = rank_bounds(count, skew)
    pick = jax.random.randint(jax.random.fold_in(key, 1), dims, 0, int(listing[count - 1]))
    grade = jnp.searchsorted(jnp.asarray(listing, jnp.int32), pick, side="right")
    return jax.random.permutation(jax.random.fold_in(key, 2), count)[grade].astype(jnp.int32)


def gaussian(rng, dims, scale, limit, cuts=(), kind=jnp.bfloat16):
    values = jax.random.normal(rng, dims, jnp.float32) * scale
    if len(cuts) > 0:
        values = steps_of(rng, dims, cuts, -0.22, 0.18) * values
    return jnp.clip(values, min=-limit, max=limit).astype(kind)


def setup_inputs(seed: int = 0) -> dict:
    splits = jax.random.split(jax.random.key(seed), 16)
    inputs_t = gaussian(splits[0], (FEATURES, INPUT_NODES), 1.0, 6.0, ((0, 4), (1, 8)))
    tiles_first = draw_tiles_first(jax.random.fold_in(splits[15], 71), 0)
    first_dst = draw_first_dst(jax.random.fold_in(splits[15], 71), 0)
    first_src = touch_ends(jax.random.randint(splits[3], (N_DOM * TILES_FIRST,), 0, INPUT_BLOCKS), jax.random.fold_in(splits[3], 1), 0, INPUT_BLOCKS - 1).astype(jnp.int32)
    w1_self = gaussian(splits[4], (FEATURES, HIDDEN_WIDTH), FEATURES ** -0.5, 0.5, ((0, 4),))
    w1_neigh = gaussian(splits[5], (FEATURES, HIDDEN_WIDTH), 1.0, 6.0, ((0, 4),))
    bias_first = gaussian(splits[6], (HIDDEN_WIDTH,), 0.5, 3.0, (), jnp.float32)
    fetch_ids = draw_fetch_ids(jax.random.fold_in(splits[15], 71), 0)
    tiles_out = draw_tiles_out(jax.random.fold_in(splits[15], 71), 0)
    out_dst = draw_out_dst(jax.random.fold_in(splits[15], 71), 0)
    out_src = draw_out_src(jax.random.fold_in(splits[15], 71), 0)
    output_self_weight = gaussian(splits[11], (HIDDEN_WIDTH, CLASSES), 0.15, 1.0)
    output_neighbour_weight = gaussian(splits[12], (HIDDEN_WIDTH, CLASSES), 0.3, 2.0)
    bias_out = gaussian(splits[13], (CLASSES,), 1.0, 4.0, (), jnp.float32)
    labels = touch_ends(ranked(splits[14], (TARGETS,), CLASSES, 2), jax.random.fold_in(splits[14], 3), 0, CLASSES - 1).astype(jnp.int32)
    return dict(inputs_t=inputs_t, tiles_first=tiles_first, first_dst=first_dst, first_src=first_src, w1_self=w1_self, w1_neigh=w1_neigh, bias_first=bias_first, fetch_ids=fetch_ids, tiles_out=tiles_out, out_dst=out_dst, out_src=out_src, output_self_weight=output_self_weight, output_neighbour_weight=output_neighbour_weight, bias_out=bias_out, labels=labels)


def tile_mean(tiles, dst_ids, src_blocks, blocks):
    product = jnp.einsum('tij,tjw->tiw', tiles.astype(jnp.float32), src_blocks.astype(jnp.float32))
    picker = (dst_ids[:, None] == jnp.arange(blocks, dtype=jnp.int32)[None, :]).astype(jnp.float32)
    summed = jnp.einsum('tb,tiw->biw', picker, product)
    weight_sum = jnp.einsum('tb,ti->bi', picker, lax.optimization_barrier(jnp.sum(tiles.astype(jnp.float32), axis=2)))
    return (summed, weight_sum)

def reference(inputs_t, tiles_first, first_dst, first_src, w1_self, w1_neigh, bias_first, fetch_ids, tiles_out, out_dst, out_src, output_self_weight, output_neighbour_weight, bias_out, labels):
    devices = N_DOM * N_FEAT
    dom_blocks = N_FEAT * BLOCKS_DEV
    rows_dom = dom_blocks * TILE_ROWS
    rows_dev = BLOCKS_DEV * TILE_ROWS
    feature_rows = inputs_t.T.reshape(N_DOM, INPUT_BLOCKS, TILE_ROWS, FEATURES)
    first_tiles = tiles_first.reshape(N_DOM, TILES_FIRST, TILE_ROWS, TILE_ROWS)
    first_dst_all = first_dst.reshape(N_DOM, TILES_FIRST)
    first_src_all = first_src.reshape(N_DOM, TILES_FIRST)

    def first_layer(pieces):
        rows_in, tile_part, dst_part, src_part = pieces
        summed, weight_sum = tile_mean(tile_part, dst_part, rows_in[src_part], dom_blocks)
        neighbour_aggregate = (summed / weight_sum[:, :, None]).reshape(rows_dom, FEATURES).astype(jnp.bfloat16)
        local_node_rows = rows_in.reshape(INPUT_BLOCKS * TILE_ROWS, FEATURES)[:rows_dom]
        pre = jnp.dot(neighbour_aggregate, w1_neigh, preferred_element_type=jnp.float32) + jnp.dot(local_node_rows, w1_self, preferred_element_type=jnp.float32) + bias_first
        return (neighbour_aggregate, local_node_rows, pre)
    agg1, self1, pre1 = lax.map(first_layer, (feature_rows, first_tiles, first_dst_all, first_src_all))
    agg1 = agg1.reshape(TARGETS, FEATURES)
    self1 = self1.reshape(TARGETS, FEATURES)
    pre1 = pre1.reshape(TARGETS, HIDDEN_WIDTH)
    hidden_units = jnp.maximum(pre1, 0.0).astype(jnp.bfloat16)
    hidden_blocks = hidden_units.reshape(devices * BLOCKS_DEV, TILE_ROWS, HIDDEN_WIDTH)
    out_tiles = tiles_out.reshape(devices, TILES_OUT, TILE_ROWS, TILE_ROWS)
    out_dst_all = out_dst.reshape(devices, TILES_OUT)
    out_src_all = out_src.reshape(devices, TILES_OUT)
    label_rows = labels.reshape(devices, rows_dev)
    owner_base = (jnp.arange(devices, dtype=jnp.int32) * BLOCKS_DEV)[:, None]
    scale = 1.0 / math.sqrt(TARGETS)

    def out_layer(state, pieces):
        back, output_self_gradient, output_neighbour_gradient, gb3 = state
        device, tile_part, dst_part, src_part, label_part, fetch_part = pieces
        slot_blocks = (owner_base + fetch_part).reshape(-1).astype(jnp.int32)
        received = hidden_blocks[slot_blocks]
        summed, weight_sum = tile_mean(tile_part, dst_part, received[src_part], BLOCKS_DEV)
        neighbour_aggregate = (summed / weight_sum[:, :, None]).reshape(rows_dev, HIDDEN_WIDTH).astype(jnp.bfloat16)
        local_node_rows = lax.dynamic_slice_in_dim(hidden_units, (device * rows_dev).astype(jnp.int32), rows_dev, 0)
        logits = jnp.dot(local_node_rows, output_self_weight, preferred_element_type=jnp.float32) + jnp.dot(neighbour_aggregate, output_neighbour_weight, preferred_element_type=jnp.float32) + bias_out
        expo = jnp.exp(logits - lax.optimization_barrier(jnp.max(logits, axis=1, keepdims=True)))
        prob = expo / lax.optimization_barrier(jnp.sum(expo, axis=1, keepdims=True))
        onehot = (label_part[:, None] == jnp.arange(CLASSES, dtype=jnp.int32)[None, :]).astype(jnp.float32)
        logits_gradient = (prob - onehot) * scale
        logit_gradient = logits_gradient.astype(jnp.bfloat16)
        output_self_gradient = output_self_gradient + jnp.dot(local_node_rows.T, logit_gradient, preferred_element_type=jnp.float32)
        output_neighbour_gradient = output_neighbour_gradient + jnp.dot(neighbour_aggregate.T, logit_gradient, preferred_element_type=jnp.float32)
        gb3 = gb3 + lax.optimization_barrier(jnp.sum(logits_gradient, axis=0))
        aggregate_gradient = jnp.dot(logit_gradient, output_neighbour_weight.T, preferred_element_type=jnp.float32)
        gnum = (aggregate_gradient.reshape(BLOCKS_DEV, TILE_ROWS, HIDDEN_WIDTH) / weight_sum[:, :, None]).astype(jnp.bfloat16)
        contrib = jnp.einsum('tji,tjw->tiw', tile_part.astype(jnp.float32), gnum[dst_part].astype(jnp.float32))
        slot_grad = jnp.zeros((devices * SLOTS_PEER, TILE_ROWS, HIDDEN_WIDTH), jnp.float32).at[src_part].add(contrib).astype(jnp.bfloat16)
        back = back.at[slot_blocks].add(slot_grad.astype(jnp.float32))
        local_gradient = jnp.dot(logit_gradient, output_self_weight.T, preferred_element_type=jnp.float32)
        return ((back, output_self_gradient, output_neighbour_gradient, gb3), local_gradient)
    start_state = (jnp.zeros((devices * BLOCKS_DEV, TILE_ROWS, HIDDEN_WIDTH), jnp.float32), jnp.zeros((HIDDEN_WIDTH, CLASSES), jnp.float32), jnp.zeros((HIDDEN_WIDTH, CLASSES), jnp.float32), jnp.zeros((CLASSES,), jnp.float32))
    (back, output_self_gradient, output_neighbour_gradient, gb3), own_grads = lax.scan(out_layer, start_state, (jnp.arange(devices, dtype=jnp.int32), out_tiles, out_dst_all, out_src_all, label_rows, fetch_ids))
    grad_hidden = back.reshape(TARGETS, HIDDEN_WIDTH) + own_grads.reshape(TARGETS, HIDDEN_WIDTH)
    grad_pre = jnp.where(pre1 > 0.0, grad_hidden, 0.0).astype(jnp.bfloat16)
    gw1s = jnp.dot(self1.T, grad_pre, preferred_element_type=jnp.float32)
    gw1n = jnp.dot(agg1.T, grad_pre, preferred_element_type=jnp.float32)
    gb1 = lax.optimization_barrier(jnp.sum(grad_pre.astype(jnp.float32), axis=0))
    return (gw1s, gw1n, gb1, output_self_gradient, output_neighbour_gradient, gb3)
```

```python
import math

import jax
import jax.numpy as jnp
from jax import lax
from jax.experimental import pallas as pl
from jax.experimental.pallas import tpu as pltpu
from jax.sharding import PartitionSpec as P

F32 = jnp.float32
BF16 = jnp.bfloat16
BIG = pltpu.CompilerParams(vmem_limit_bytes=58 << 20)
VMEM = pl.BlockSpec(memory_space=pltpu.VMEM)


def group_of(count, most):
    return math.gcd(count, most)


def first_layer(features_t, tiles, dst_ids, src_ids, blocks, owners):
    width, nodes = features_t.shape
    total, side, _ = tiles.shape
    step = group_of(total, 32)
    unroll = group_of(step, 16)
    steps = total // step
    per_owner = blocks // owners

    def kernel(dst_s, src_s, tile_ref, feat_ref, out_ref, acc):
        i = pl.program_id(0)

        @pl.when(i == 0)
        def _():
            acc[...] = jnp.zeros_like(acc)

        ones = jnp.ones((16, side), BF16)

        def body(g, carry):
            products = []
            for u in range(unroll):
                t = g * unroll + u
                start = pl.multiple_of(src_s[i * step + t] * side, side)
                left = jnp.concatenate([feat_ref[:, pl.ds(start, side)], ones], axis=0)
                products.append(
                    lax.dot_general(
                        left, tile_ref[t], (((1,), (1,)), ((), ())), preferred_element_type=F32
                    )
                )
            for u in range(unroll):
                acc[dst_s[i * step + g * unroll + u]] += products[u]
            return carry

        lax.fori_loop(0, step // unroll, body, 0)

        @pl.when(i == steps - 1)
        def _():
            for q in range(owners):
                for b in range(per_owner):
                    block = acc[q * per_owner + b]
                    mean = block[:width] / block[width : width + 1]
                    out_ref[q, :width, b * side : (b + 1) * side] = mean.astype(BF16)
                rows = per_owner * side
                out_ref[q, width:, :] = feat_ref[:, q * rows : (q + 1) * rows]

    shape = (owners, 2 * width, per_owner * side)
    return pl.pallas_call(
        kernel,
        grid_spec=pltpu.PrefetchScalarGridSpec(
            num_scalar_prefetch=2,
            grid=(steps,),
            in_specs=[
                pl.BlockSpec((step, side, side), lambda i, *_: (i, 0, 0)),
                pl.BlockSpec((width, nodes), lambda i, *_: (0, 0)),
            ],
            out_specs=pl.BlockSpec(shape, lambda i, *_: (0, 0, 0)),
            scratch_shapes=[pltpu.VMEM((blocks, width + 16, side), F32)],
        ),
        out_shape=jax.ShapeDtypeStruct(shape, BF16),
        compiler_params=BIG,
        name="first_layer",
    )(dst_ids, src_ids, tiles, features_t)


def hidden_layer(parts_t, weights, bias):
    rows = parts_t.shape[1]
    width = weights.shape[1]

    def kernel(parts_ref, w_ref, b_ref, pre_ref, hidden_ref):
        pre = (
            lax.dot_general(
                parts_ref[...], w_ref[...], (((0,), (0,)), ((), ())), preferred_element_type=F32
            )
            + b_ref[...]
        )
        pre_ref[...] = pre
        hidden_ref[...] = jnp.maximum(pre, 0.0).astype(BF16)

    return pl.pallas_call(
        kernel,
        in_specs=[VMEM] * 3,
        out_specs=[VMEM] * 2,
        out_shape=[
            jax.ShapeDtypeStruct((rows, width), F32),
            jax.ShapeDtypeStruct((rows, width), BF16),
        ],
        compiler_params=BIG,
        name="hidden_layer",
    )(parts_t, weights, bias)


def row_weights(tiles, dst_ids, blocks):
    total, side, _ = tiles.shape
    step = group_of(total, 32)
    unroll = group_of(step, 8)
    steps = total // step

    def kernel(dst_s, tile_ref, out_ref, acc):
        i = pl.program_id(0)

        @pl.when(i == 0)
        def _():
            acc[...] = jnp.zeros_like(acc)

        def body(g, carry):
            for u in range(unroll):
                t = g * unroll + u
                acc[dst_s[i * step + t]] += tile_ref[t].astype(F32)
            return carry

        lax.fori_loop(0, step // unroll, body, 0)

        @pl.when(i == steps - 1)
        def _():
            for b in range(blocks):
                out_ref[b] = jnp.broadcast_to(
                    jnp.sum(acc[b], axis=1, keepdims=True), (side, side)
                )

    return pl.pallas_call(
        kernel,
        grid_spec=pltpu.PrefetchScalarGridSpec(
            num_scalar_prefetch=1,
            grid=(steps,),
            in_specs=[pl.BlockSpec((step, side, side), lambda i, *_: (i, 0, 0))],
            out_specs=pl.BlockSpec((blocks, side, side), lambda i, *_: (0, 0, 0)),
            scratch_shapes=[pltpu.VMEM((blocks, side, side), F32)],
        ),
        out_shape=jax.ShapeDtypeStruct((blocks, side, side), F32),
        compiler_params=BIG,
        cost_estimate=pl.CostEstimate(
            flops=2 * total * side * side, bytes_accessed=2 * total * side * side, transcendentals=0
        ),
        name="row_weights",
    )(dst_ids, tiles)


def output_layer(
    tiles, dst_ids, src_ids, pool, weight, hidden, w_self, w_neigh, bias, labels, scale
):
    total, side, _ = tiles.shape
    blocks = weight.shape[0]
    width = pool.shape[2]
    classes = w_self.shape[1]
    step = group_of(total, 32)
    unroll = group_of(step, 32)
    steps = total // step
    lead = (((0,), (0,)), ((), ()))
    last = (((1,), (1,)), ((), ()))

    def kernel(
        dst_s, src_s, tile_ref, pool_ref, weight_ref, hidden_ref, ws_ref, wn_ref, bias_ref,
        labels_ref, gws_ref, gwn_ref, gb_ref, gnum_ref, own_ref, acc,
    ):
        i = pl.program_id(0)

        @pl.when(i == 0)
        def _():
            acc[...] = jnp.zeros_like(acc)

        def body(g, carry):
            products = []
            for u in range(unroll):
                t = g * unroll + u
                products.append(
                    jnp.dot(tile_ref[t], pool_ref[src_s[i * step + t]], preferred_element_type=F32)
                )
            for u in range(unroll):
                acc[dst_s[i * step + g * unroll + u]] += products[u]
            return carry

        lax.fori_loop(0, step // unroll, body, 0)

        @pl.when(i == steps - 1)
        def _():
            gws = jnp.zeros((width, classes), F32)
            gwn = jnp.zeros((width, classes), F32)
            gb = jnp.zeros((1, classes), F32)
            for b in range(blocks):
                rows = slice(b * side, (b + 1) * side)
                under = weight_ref[b][:, :1]
                mean = (acc[b] / under).astype(BF16)
                own = hidden_ref[rows, :]
                logits = (
                    jnp.dot(own, ws_ref[...], preferred_element_type=F32)
                    + jnp.dot(mean, wn_ref[...], preferred_element_type=F32)
                    + bias_ref[...]
                )
                expo = jnp.exp(logits - jnp.max(logits, axis=1, keepdims=True))
                prob = expo / jnp.sum(expo, axis=1, keepdims=True)
                lane = lax.broadcasted_iota(jnp.int32, (side, classes), 1)
                onehot = jnp.where(labels_ref[rows, :] == lane, 1.0, 0.0)
                grad = (prob - onehot) * scale
                glog = grad.astype(BF16)
                gb = gb + jnp.sum(grad, axis=0, keepdims=True)
                gws = gws + lax.dot_general(own, glog, lead, preferred_element_type=F32)
                gwn = gwn + lax.dot_general(mean, glog, lead, preferred_element_type=F32)
                back = lax.dot_general(glog, wn_ref[...], last, preferred_element_type=F32)
                gnum_ref[b] = (back / under).astype(BF16)
                own_ref[rows, :] = lax.dot_general(
                    glog, ws_ref[...], last, preferred_element_type=F32
                )
            gws_ref[...] = gws
            gwn_ref[...] = gwn
            gb_ref[...] = gb

    def whole(*shape):
        return pl.BlockSpec(shape, lambda i, *_: (0,) * len(shape))

    rows = blocks * side
    out = [
        ((width, classes), F32),
        ((width, classes), F32),
        ((1, classes), F32),
        ((blocks, side, width), BF16),
        ((rows, width), F32),
    ]
    return pl.pallas_call(
        kernel,
        grid_spec=pltpu.PrefetchScalarGridSpec(
            num_scalar_prefetch=2,
            grid=(steps,),
            in_specs=[
                pl.BlockSpec((step, side, side), lambda i, *_: (i, 0, 0)),
                pl.BlockSpec(memory_space=pltpu.VMEM),
                whole(blocks, side, side),
                whole(rows, width),
                whole(width, classes),
                whole(width, classes),
                whole(1, classes),
                whole(rows, 1),
            ],
            out_specs=[whole(*s) for s, _ in out],
            scratch_shapes=[pltpu.VMEM((blocks, side, width), F32)],
        ),
        out_shape=[jax.ShapeDtypeStruct(s, d) for s, d in out],
        compiler_params=BIG,
        name="output_layer",
    )(
        dst_ids, src_ids, tiles, pool, weight, hidden, w_self, w_neigh,
        bias.reshape(1, classes), labels.reshape(rows, 1),
    )


def slot_gradients(tiles, dst_ids, src_ids, gnum, slots):
    total, side, _ = tiles.shape
    width = gnum.shape[2]
    step = group_of(total, 32)
    unroll = group_of(step, 32)
    steps = total // step
    piece = group_of(slots, 8)

    def kernel(dst_s, src_s, tile_ref, gnum_ref, out_ref, acc):
        i = pl.program_id(0)

        @pl.when(i == 0)
        def _():
            acc[...] = jnp.zeros_like(acc)

        @pl.when(i < steps)
        def _():
            def body(g, carry):
                products = []
                for u in range(unroll):
                    t = g * unroll + u
                    products.append(
                        lax.dot_general(
                            tile_ref[t], gnum_ref[dst_s[i * step + t]],
                            (((0,), (0,)), ((), ())), preferred_element_type=F32,
                        )
                    )
                for u in range(unroll):
                    acc[src_s[i * step + g * unroll + u]] += products[u]
                return carry

            lax.fori_loop(0, step // unroll, body, 0)

        @pl.when(i >= steps)
        def _():
            out_ref[...] = acc[pl.ds((i - steps) * piece, piece)].astype(BF16)

    return pl.pallas_call(
        kernel,
        grid_spec=pltpu.PrefetchScalarGridSpec(
            num_scalar_prefetch=2,
            grid=(steps + slots // piece,),
            in_specs=[
                pl.BlockSpec(
                    (step, side, side), lambda i, *_: (jnp.minimum(i, steps - 1), 0, 0)
                ),
                pl.BlockSpec(gnum.shape, lambda i, *_: (0, 0, 0)),
            ],
            out_specs=pl.BlockSpec(
                (piece, side, width), lambda i, *_: (jnp.maximum(i - steps, 0), 0, 0)
            ),
            scratch_shapes=[pltpu.VMEM((slots, side, width), F32)],
        ),
        out_shape=jax.ShapeDtypeStruct((slots, side, width), BF16),
        compiler_params=BIG,
        name="slot_gradients",
    )(dst_ids, src_ids, tiles, gnum)


def first_gradients(returned, wanted, own, pre, parts_t):
    slots, side, width = returned.shape
    rows = own.shape[0]
    blocks = rows // side
    features = parts_t.shape[0]
    step = group_of(slots, 16)
    steps = slots // step

    def kernel(want_s, ret_ref, own_ref, pre_ref, parts_ref, gw_ref, gb_ref, acc):
        i = pl.program_id(0)

        @pl.when(i == 0)
        def _():
            acc[...] = jnp.zeros_like(acc)

        for s in range(step):
            acc[want_s[i * step + s]] += ret_ref[s].astype(F32)

        @pl.when(i == steps - 1)
        def _():
            grad = acc[...].reshape(rows, width) + own_ref[...]
            grad_pre = jnp.where(pre_ref[...] > 0.0, grad, 0.0).astype(BF16)
            gb = jnp.sum(grad_pre.astype(F32), axis=0, keepdims=True)
            gb_ref[...] = jnp.broadcast_to(gb, gb_ref.shape)
            gw_ref[...] = jnp.dot(parts_ref[...], grad_pre, preferred_element_type=F32)

    def whole(*shape):
        return pl.BlockSpec(shape, lambda i, *_: (0,) * len(shape))

    return pl.pallas_call(
        kernel,
        grid_spec=pltpu.PrefetchScalarGridSpec(
            num_scalar_prefetch=1,
            grid=(steps,),
            in_specs=[
                pl.BlockSpec((step, side, width), lambda i, *_: (i, 0, 0)),
                whole(rows, width),
                whole(rows, width),
                whole(*parts_t.shape),
            ],
            out_specs=[whole(features, width), whole(8, width)],
            scratch_shapes=[pltpu.VMEM((blocks, side, width), F32)],
        ),
        out_shape=[
            jax.ShapeDtypeStruct((features, width), F32),
            jax.ShapeDtypeStruct((8, width), F32),
        ],
        compiler_params=BIG,
        name="first_gradients",
    )(wanted, returned, own, pre, parts_t)


def doubling_sum(value, axis):
    size = lax.axis_size(axis)
    reach = 1
    while reach < size:
        value = value + lax.ppermute(value, axis, [(k, k ^ reach) for k in range(size)])
        reach *= 2
    return value


def on_device(
    inputs_t, tiles_first, first_dst, first_src, w1_self, w1_neigh, bias_first, fetch_ids,
    tiles_out, out_dst, out_src, output_self_weight, output_neighbour_weight, bias_out, labels,
):
    every = ("dom", "feat")
    n_feat = lax.axis_size("feat")
    devices = lax.axis_size("dom") * n_feat
    side = tiles_out.shape[1]
    rows_dev = labels.shape[0]
    blocks = rows_dev // side
    slots_peer = fetch_ids.shape[2]
    features, width = w1_self.shape
    classes = output_self_weight.shape[1]
    scale = 1.0 / math.sqrt(devices * rows_dev)

    weights = lax.all_gather(jnp.concatenate([w1_neigh, w1_self]), "feat", axis=0, tiled=True)
    parts = first_layer(inputs_t, tiles_first, first_dst, first_src, n_feat * blocks, n_feat)
    parts = lax.all_to_all(parts, "feat", split_axis=0, concat_axis=0, tiled=True)
    parts_t = parts.reshape(n_feat * 2 * features, rows_dev)
    pre, hidden = hidden_layer(parts_t, weights, bias_first.reshape(1, width))
    wanted = fetch_ids[:, 0, :]
    outgoing = hidden.reshape(blocks, side, width)[wanted]
    pool = lax.all_to_all(outgoing, every, split_axis=0, concat_axis=0, tiled=True)
    pool = pool.reshape(devices * slots_peer, side, width)
    weight = row_weights(tiles_out, out_dst, blocks)
    gws, gwn, gb3, gnum, own = output_layer(
        tiles_out, out_dst, out_src, pool, weight, hidden, output_self_weight,
        output_neighbour_weight, bias_out, labels, scale,
    )
    part = jnp.concatenate([gws, gwn], axis=0)
    part = part.reshape(devices, 2 * width // devices, classes)
    part = lax.all_to_all(part, every, split_axis=0, concat_axis=0, tiled=True)
    both = lax.all_gather(jnp.sum(part, axis=0), every, axis=0, tiled=True)
    slot_grad = slot_gradients(tiles_out, out_dst, out_src, gnum, devices * slots_peer)
    slot_grad = slot_grad.reshape(devices, slots_peer, side, width)
    returned = lax.all_to_all(slot_grad, every, split_axis=0, concat_axis=0, tiled=True)
    gw1, gb1 = first_gradients(
        returned.reshape(devices * slots_peer, side, width), wanted.reshape(-1), own, pre, parts_t
    )
    row = jnp.zeros((1, width), F32).at[:, :classes].set(gb3)
    small = jnp.concatenate([gb1[:1], row, jnp.zeros((6, width), F32)])
    small = jnp.broadcast_to(small, (n_feat, 8, width))
    last = jnp.concatenate([gw1.reshape(n_feat, 2 * features, width), small], axis=1)
    last = lax.all_to_all(last, "feat", split_axis=0, concat_axis=0, tiled=True)
    last = doubling_sum(jnp.sum(last, axis=0), "dom")
    edge = 2 * features
    return (
        last[features:edge],
        last[:features],
        last[edge],
        both[:width],
        both[width:],
        last[edge + 1, :classes],
    )


def solution(mesh):
    in_specs = (
        P("feat", "dom"),
        P("dom", None, None),
        P("dom"),
        P("dom"),
        P("feat", None),
        P("feat", None),
        P(),
        P(None, ("dom", "feat"), None),
        P(("dom", "feat"), None, None),
        P(("dom", "feat")),
        P(("dom", "feat")),
        P(),
        P(),
        P(),
        P(("dom", "feat")),
    )
    out_specs = (P("feat", None), P("feat", None), P(), P(), P(), P())
    return jax.shard_map(
        on_device, mesh=mesh, in_specs=in_specs, out_specs=out_specs, check_vma=False
    )
```

```python
import math

import jax
import jax.numpy as jnp
from jax import lax
from jax.experimental import pallas as pl
from jax.experimental.pallas import tpu as pltpu
from jax.sharding import PartitionSpec as P

F32 = jnp.float32
BF16 = jnp.bfloat16
BIG = pltpu.CompilerParams(vmem_limit_bytes=58 << 20)
VMEM = pl.BlockSpec(memory_space=pltpu.VMEM)


def group_of(count, most):
    return math.gcd(count, most)


def first_layer(features_t, tiles, dst_ids, src_ids, me, blocks, owners):
    width, nodes = features_t.shape
    total, side, _ = tiles.shape
    step = group_of(total, 32)
    unroll = group_of(step, 16)
    steps = total // step
    per_owner = blocks // owners

    def kernel(dst_s, src_s, me_s, tile_ref, feat_ref, *refs):
        outs, acc = refs[:-1], refs[-1]
        i = pl.program_id(0)

        @pl.when(i == 0)
        def _():
            acc[...] = jnp.zeros_like(acc)

        ones = jnp.ones((16, side), BF16)

        def body(g, carry):
            products = []
            for u in range(unroll):
                t = g * unroll + u
                start = pl.multiple_of(src_s[i * step + t] * side, side)
                left = jnp.concatenate([feat_ref[:, pl.ds(start, side)], ones], axis=0)
                products.append(
                    lax.dot_general(
                        left, tile_ref[t], (((1,), (1,)), ((), ())), preferred_element_type=F32
                    )
                )
            for u in range(unroll):
                acc[dst_s[i * step + g * unroll + u]] += products[u]
            return carry

        lax.fori_loop(0, step // unroll, body, 0)

        @pl.when(i == steps - 1)
        def _():
            rows = per_owner * side
            for r in range(owners):
                q = me_s[0] ^ r
                for b in range(per_owner):
                    block = acc[q * per_owner + b]
                    mean = block[:width] / block[width : width + 1]
                    outs[r][:width, b * side : (b + 1) * side] = mean.astype(BF16)
                outs[r][width:, :] = feat_ref[:, pl.ds(pl.multiple_of(q * rows, side), rows)]

    shape = (2 * width, per_owner * side)
    return pl.pallas_call(
        kernel,
        grid_spec=pltpu.PrefetchScalarGridSpec(
            num_scalar_prefetch=3,
            grid=(steps,),
            in_specs=[
                pl.BlockSpec((step, side, side), lambda i, *_: (i, 0, 0)),
                pl.BlockSpec((width, nodes), lambda i, *_: (0, 0)),
            ],
            out_specs=[pl.BlockSpec(shape, lambda i, *_: (0, 0))] * owners,
            scratch_shapes=[pltpu.VMEM((blocks, width + 16, side), F32)],
        ),
        out_shape=[jax.ShapeDtypeStruct(shape, BF16)] * owners,
        compiler_params=BIG,
        name="first_layer",
    )(dst_ids, src_ids, me, tiles, features_t)


def hidden_layer(parts, weights, bias):
    count = len(parts)
    rows = parts[0].shape[1]
    width = weights[0].shape[1]

    def kernel(*refs):
        b_ref, pre_ref, hidden_ref = refs[2 * count :]
        pre = jnp.zeros((rows, width), F32)
        for r in range(count):
            pre = pre + lax.dot_general(
                refs[r][...], refs[count + r][...], (((0,), (0,)), ((), ())),
                preferred_element_type=F32,
            )
        pre = pre + b_ref[...]
        pre_ref[...] = pre
        hidden_ref[...] = jnp.maximum(pre, 0.0).astype(BF16)

    return pl.pallas_call(
        kernel,
        in_specs=[VMEM] * (2 * count + 1),
        out_specs=[VMEM] * 2,
        out_shape=[
            jax.ShapeDtypeStruct((rows, width), F32),
            jax.ShapeDtypeStruct((rows, width), BF16),
        ],
        compiler_params=BIG,
        name="hidden_layer",
    )(*parts, *weights, bias)


def row_weights(tiles, dst_ids, blocks):
    total, side, _ = tiles.shape
    step = group_of(total, 32)
    unroll = group_of(step, 8)
    steps = total // step

    def kernel(dst_s, tile_ref, out_ref, acc):
        i = pl.program_id(0)

        @pl.when(i == 0)
        def _():
            acc[...] = jnp.zeros_like(acc)

        def body(g, carry):
            for u in range(unroll):
                t = g * unroll + u
                acc[dst_s[i * step + t]] += tile_ref[t].astype(F32)
            return carry

        lax.fori_loop(0, step // unroll, body, 0)

        @pl.when(i == steps - 1)
        def _():
            for b in range(blocks):
                out_ref[b] = jnp.broadcast_to(
                    jnp.sum(acc[b], axis=1, keepdims=True), (side, side)
                )

    return pl.pallas_call(
        kernel,
        grid_spec=pltpu.PrefetchScalarGridSpec(
            num_scalar_prefetch=1,
            grid=(steps,),
            in_specs=[pl.BlockSpec((step, side, side), lambda i, *_: (i, 0, 0))],
            out_specs=pl.BlockSpec((blocks, side, side), lambda i, *_: (0, 0, 0)),
            scratch_shapes=[pltpu.VMEM((blocks, side, side), F32)],
        ),
        out_shape=jax.ShapeDtypeStruct((blocks, side, side), F32),
        compiler_params=BIG,
        cost_estimate=pl.CostEstimate(
            flops=2 * total * side * side, bytes_accessed=2 * total * side * side, transcendentals=0
        ),
        name="row_weights",
    )(dst_ids, tiles)


def output_layer(
    tiles, dst_ids, src_ids, place, me, pools, weight, hidden, w_self, w_neigh, bias, labels,
    scale, n_feat,
):
    total, side, _ = tiles.shape
    blocks = weight.shape[0]
    width = hidden.shape[1]
    count = len(pools)
    per_pool = pools[0].shape[0]
    unit = 8 * n_feat
    share = -(-(2 * width + 8) // unit) * 8
    half = n_feat // 2
    classes = w_self.shape[1]
    step = group_of(total, 32)
    unroll = group_of(step, 32)
    steps = total // step
    lead = (((0,), (0,)), ((), ()))
    last = (((1,), (1,)), ((), ()))

    def kernel(
        dst_s, src_s, place_s, me_s, tile_ref, weight_ref, hidden_ref, ws_ref, wn_ref, bias_ref,
        labels_ref, *refs,
    ):
        pool_refs = refs[:count]
        even_ref, odd_ref, gnum_ref, own_ref, acc, pool_ref, sums, sems = refs[count:]
        i = pl.program_id(0)

        @pl.when(i == 0)
        def _():
            copies = [
                pltpu.make_async_copy(
                    pool_refs[j], pool_ref.at[pl.ds(j * per_pool, per_pool)], sems.at[j]
                )
                for j in range(count)
            ]
            for copy in copies:
                copy.start()
            acc[...] = jnp.zeros_like(acc)
            sums[...] = jnp.zeros_like(sums)
            for copy in copies:
                copy.wait()

        def body(g, carry):
            products = []
            for u in range(unroll):
                t = g * unroll + u
                products.append(
                    jnp.dot(
                        tile_ref[t],
                        pool_ref[place_s[src_s[i * step + t]]],
                        preferred_element_type=F32,
                    )
                )
            for u in range(unroll):
                acc[dst_s[i * step + g * unroll + u]] += products[u]
            return carry

        lax.fori_loop(0, step // unroll, body, 0)

        @pl.when(i == steps - 1)
        def _():
            gws = jnp.zeros((width, classes), F32)
            gwn = jnp.zeros((width, classes), F32)
            gb = jnp.zeros((1, classes), F32)
            for b in range(blocks):
                rows = slice(b * side, (b + 1) * side)
                under = weight_ref[b][:, :1]
                mean = (acc[b] / under).astype(BF16)
                own = hidden_ref[rows, :]
                logits = (
                    jnp.dot(own, ws_ref[...], preferred_element_type=F32)
                    + jnp.dot(mean, wn_ref[...], preferred_element_type=F32)
                    + bias_ref[...]
                )
                expo = jnp.exp(logits - jnp.max(logits, axis=1, keepdims=True))
                prob = expo / jnp.sum(expo, axis=1, keepdims=True)
                lane = lax.broadcasted_iota(jnp.int32, (side, classes), 1)
                onehot = jnp.where(labels_ref[rows, :] == lane, 1.0, 0.0)
                grad = (prob - onehot) * scale
                glog = grad.astype(BF16)
                gb = gb + jnp.sum(grad, axis=0, keepdims=True)
                gws = gws + lax.dot_general(own, glog, lead, preferred_element_type=F32)
                gwn = gwn + lax.dot_general(mean, glog, lead, preferred_element_type=F32)
                back = lax.dot_general(glog, wn_ref[...], last, preferred_element_type=F32)
                gnum_ref[b] = (back / under).astype(BF16)
                own_ref[rows, :] = lax.dot_general(
                    glog, ws_ref[...], last, preferred_element_type=F32
                )
            sums[:width, :] = gws
            sums[width : 2 * width, :] = gwn
            sums[2 * width : 2 * width + 8, :] = jnp.broadcast_to(gb, (8, classes))
            for r in range(n_feat):
                start = pl.multiple_of((me_s[0] ^ r) * share, 8)
                target = odd_ref if r % 2 else even_ref
                target[r // 2] = sums[pl.ds(start, share), :]

    def whole(*shape):
        return pl.BlockSpec(shape, lambda i, *_: (0,) * len(shape))

    rows = blocks * side
    out = [
        ((half, share, classes), F32),
        ((half, share, classes), F32),
        ((blocks, side, width), BF16),
        ((rows, width), F32),
    ]
    return pl.pallas_call(
        kernel,
        grid_spec=pltpu.PrefetchScalarGridSpec(
            num_scalar_prefetch=4,
            grid=(steps,),
            in_specs=[
                pl.BlockSpec((step, side, side), lambda i, *_: (i, 0, 0)),
                whole(blocks, side, side),
                whole(rows, width),
                whole(width, classes),
                whole(width, classes),
                whole(1, classes),
                whole(rows, 1),
            ]
            + [pl.BlockSpec(memory_space=pl.ANY)] * count,
            out_specs=[whole(*s) for s, _ in out],
            scratch_shapes=[
                pltpu.VMEM((blocks, side, width), F32),
                pltpu.VMEM((count * per_pool, side, width), BF16),
                pltpu.VMEM((n_feat * share, classes), F32),
                pltpu.SemaphoreType.DMA((count,)),
            ],
        ),
        out_shape=[jax.ShapeDtypeStruct(s, d) for s, d in out],
        compiler_params=BIG,
        name="output_layer",
    )(
        dst_ids, src_ids, place, me, tiles, weight, hidden, w_self, w_neigh,
        bias.reshape(1, classes), labels.reshape(rows, 1), *pools,
    )


def slot_gradients(tiles, dst_ids, src_ids, gnum, slots):
    total, side, _ = tiles.shape
    width = gnum.shape[2]
    step = group_of(total, 32)
    unroll = group_of(step, 32)
    steps = total // step
    piece = group_of(slots, 8)

    def kernel(dst_s, src_s, tile_ref, gnum_ref, out_ref, acc):
        i = pl.program_id(0)

        @pl.when(i == 0)
        def _():
            acc[...] = jnp.zeros_like(acc)

        @pl.when(i < steps)
        def _():
            def body(g, carry):
                products = []
                for u in range(unroll):
                    t = g * unroll + u
                    products.append(
                        lax.dot_general(
                            tile_ref[t], gnum_ref[dst_s[i * step + t]],
                            (((0,), (0,)), ((), ())), preferred_element_type=F32,
                        )
                    )
                for u in range(unroll):
                    acc[src_s[i * step + g * unroll + u]] += products[u]
                return carry

            lax.fori_loop(0, step // unroll, body, 0)

        @pl.when(i >= steps)
        def _():
            out_ref[...] = acc[pl.ds((i - steps) * piece, piece)].astype(BF16)

    return pl.pallas_call(
        kernel,
        grid_spec=pltpu.PrefetchScalarGridSpec(
            num_scalar_prefetch=2,
            grid=(steps + slots // piece,),
            in_specs=[
                pl.BlockSpec(
                    (step, side, side), lambda i, *_: (jnp.minimum(i, steps - 1), 0, 0)
                ),
                pl.BlockSpec(gnum.shape, lambda i, *_: (0, 0, 0)),
            ],
            out_specs=pl.BlockSpec(
                (piece, side, width), lambda i, *_: (jnp.maximum(i - steps, 0), 0, 0)
            ),
            scratch_shapes=[pltpu.VMEM((slots, side, width), F32)],
        ),
        out_shape=jax.ShapeDtypeStruct((slots, side, width), BF16),
        compiler_params=BIG,
        name="slot_gradients",
    )(dst_ids, src_ids, tiles, gnum)


def first_gradients(returned, wanted, own, pre, parts):
    slots, side, width = returned.shape
    rows = own.shape[0]
    blocks = rows // side
    count = len(parts)
    features = parts[0].shape[0]
    step = group_of(slots, 16)
    steps = slots // step

    def kernel(want_s, ret_ref, own_ref, pre_ref, *refs):
        even_ref, odd_ref, acc = refs[count:]
        i = pl.program_id(0)

        @pl.when(i == 0)
        def _():
            acc[...] = jnp.zeros_like(acc)

        for s in range(step):
            acc[want_s[i * step + s]] += ret_ref[s].astype(F32)

        @pl.when(i == steps - 1)
        def _():
            grad = acc[...].reshape(rows, width) + own_ref[...]
            grad_pre = jnp.where(pre_ref[...] > 0.0, grad, 0.0).astype(BF16)
            gb = jnp.sum(grad_pre.astype(F32), axis=0, keepdims=True)
            for r in range(count):
                target = odd_ref if r % 2 else even_ref
                target[r // 2, :features] = jnp.dot(
                    refs[r][...], grad_pre, preferred_element_type=F32
                )
                target[r // 2, features:] = jnp.broadcast_to(gb, (8, width))

    def whole(*shape):
        return pl.BlockSpec(shape, lambda i, *_: (0,) * len(shape))

    shape = (count // 2, features + 8, width)
    return pl.pallas_call(
        kernel,
        grid_spec=pltpu.PrefetchScalarGridSpec(
            num_scalar_prefetch=1,
            grid=(steps,),
            in_specs=[
                pl.BlockSpec((step, side, width), lambda i, *_: (i, 0, 0)),
                whole(rows, width),
                whole(rows, width),
            ]
            + [whole(features, rows)] * count,
            out_specs=[whole(*shape)] * 2,
            scratch_shapes=[pltpu.VMEM((blocks, side, width), F32)],
        ),
        out_shape=[jax.ShapeDtypeStruct(shape, F32)] * 2,
        compiler_params=BIG,
        name="first_gradients",
    )(wanted, returned, own, pre, *parts)


def swap(value, axis, mask):
    return lax.ppermute(value, axis, [(k, k ^ mask) for k in range(lax.axis_size(axis))])


def feat_sum(even, odd):
    value = even + swap(odd, "feat", 1)
    mask = 2
    while value.shape[0] > 1:
        value = value[0::2] + swap(value[1::2], "feat", mask)
        mask *= 2
    return value[0]


def gather_blocks(value, planes, across):
    n_dom = lax.axis_size("dom")
    down = lax.axis_size("feat") // 2
    held = []
    shifted = [value] + [swap(value, "dom", across * k) for k in range(1, planes)]
    for k, own in enumerate(shifted):
        aside = [own] + [swap(own, "dom", i) for i in range(1, across)]
        below = [own] + [swap(own, "feat", 2 * j) for j in range(1, down)]
        pieces = list(aside)
        for j in range(1, down):
            pieces.append(below[j])
            for i in range(1, across):
                if k % 2 == 0:
                    pieces.append(swap(aside[i], "feat", 2 * j))
                else:
                    pieces.append(swap(below[j], "dom", i))
        held.append(jnp.concatenate(pieces))
    return held + [swap(piece, "feat", 1) for piece in held]


def doubling_sum(value, axis):
    size = lax.axis_size(axis)
    reach = 1
    while reach < size:
        value = value + swap(value, axis, reach)
        reach *= 2
    return value


def on_device(
    inputs_t, tiles_first, first_dst, first_src, w1_self, w1_neigh, bias_first, fetch_ids,
    tiles_out, out_dst, out_src, output_self_weight, output_neighbour_weight, bias_out, labels,
):
    every = ("dom", "feat")
    n_feat = lax.axis_size("feat")
    devices = lax.axis_size("dom") * n_feat
    side = tiles_out.shape[1]
    rows_dev = labels.shape[0]
    blocks = rows_dev // side
    slots_peer = fetch_ids.shape[2]
    features, width = w1_self.shape
    classes = output_self_weight.shape[1]
    scale = 1.0 / math.sqrt(devices * rows_dev)

    me_dom, me_feat = lax.axis_index("dom"), lax.axis_index("feat")
    me = me_feat.astype(jnp.int32).reshape(1)
    planes = math.gcd(lax.axis_size("dom"), 4)
    across = lax.axis_size("dom") // planes

    weights = jnp.concatenate([w1_neigh, w1_self])
    weights = [weights] + [swap(weights, "feat", r) for r in range(1, n_feat)]
    parts = first_layer(inputs_t, tiles_first, first_dst, first_src, me, n_feat * blocks, n_feat)
    parts = [parts[0]] + [swap(parts[r], "feat", r) for r in range(1, n_feat)]
    pre, hidden = hidden_layer(parts, weights, bias_first.reshape(1, width))
    wanted = fetch_ids[:, 0, :]
    pools = gather_blocks(hidden, planes, across)
    pools = [pool.reshape(-1, side, width) for pool in pools]
    owner = jnp.arange(devices, dtype=jnp.int32)[:, None]
    off_dom = (owner // n_feat) ^ me_dom
    off_feat = (owner % n_feat) ^ me_feat
    place = (off_feat % 2) * planes + off_dom // across
    place = (place * (n_feat // 2) + off_feat // 2) * across + off_dom % across
    lists = lax.all_gather(wanted.reshape(1, -1), every, axis=0, tiled=True)
    index = (me_dom * n_feat + me_feat) * slots_peer
    mine = lax.dynamic_slice_in_dim(lists, index, slots_peer, axis=1)
    place = (place * blocks + mine).reshape(-1)
    weight = row_weights(tiles_out, out_dst, blocks)
    even, odd, gnum, own = output_layer(
        tiles_out, out_dst, out_src, place, me, pools, weight, hidden, output_self_weight,
        output_neighbour_weight, bias_out, labels, scale, n_feat,
    )
    third = doubling_sum(feat_sum(even, odd), "dom")
    third = jnp.stack([third] + [swap(third, "feat", r) for r in range(1, n_feat)])
    third = jnp.take(third, jnp.arange(n_feat) ^ me_feat, axis=0).reshape(-1, classes)
    slot_grad = slot_gradients(tiles_out, out_dst, out_src, gnum, devices * slots_peer)
    slot_grad = slot_grad.reshape(devices, slots_peer, side, width)
    returned = lax.all_to_all(slot_grad, every, split_axis=0, concat_axis=0, tiled=True)
    even, odd = first_gradients(
        returned.reshape(devices * slots_peer, side, width), wanted.reshape(-1), own, pre, parts
    )
    last = doubling_sum(feat_sum(even, odd), "dom")
    edge = 2 * features
    return (
        last[features:edge],
        last[:features],
        last[edge],
        third[:width],
        third[width : 2 * width],
        third[2 * width],
    )


def solution(mesh):
    in_specs = (
        P("feat", "dom"),
        P("dom", None, None),
        P("dom"),
        P("dom"),
        P("feat", None),
        P("feat", None),
        P(),
        P(None, ("dom", "feat"), None),
        P(("dom", "feat"), None, None),
        P(("dom", "feat")),
        P(("dom", "feat")),
        P(),
        P(),
        P(),
        P(("dom", "feat")),
    )
    out_specs = (P("feat", None), P("feat", None), P(), P(), P(), P())
    return jax.shard_map(
        on_device, mesh=mesh, in_specs=in_specs, out_specs=out_specs, check_vma=False
    )
```

```python
import math

import jax
import jax.numpy as jnp
from jax import lax
from jax.experimental import pallas as pl
from jax.experimental.pallas import tpu as pltpu
from jax.sharding import PartitionSpec as P

F32 = jnp.float32
BF16 = jnp.bfloat16
BIG = pltpu.CompilerParams(vmem_limit_bytes=58 << 20)
VMEM = pl.BlockSpec(memory_space=pltpu.VMEM)


def group_of(count, most):
    return math.gcd(count, most)


def first_layer(features_t, tiles, dst_ids, src_ids, me, blocks, owners):
    width, nodes = features_t.shape
    total, side, _ = tiles.shape
    step = group_of(total, 32)
    unroll = group_of(step, 16)
    steps = total // step
    per_owner = blocks // owners

    def kernel(dst_s, src_s, me_s, tile_ref, feat_ref, *refs):
        outs, acc = refs[:-1], refs[-1]
        i = pl.program_id(0)

        @pl.when(i == 0)
        def _():
            acc[...] = jnp.zeros_like(acc)

        ones = jnp.ones((16, side), BF16)

        def body(g, carry):
            products = []
            for u in range(unroll):
                t = g * unroll + u
                start = pl.multiple_of(src_s[i * step + t] * side, side)
                left = jnp.concatenate([feat_ref[:, pl.ds(start, side)], ones], axis=0)
                products.append(
                    lax.dot_general(
                        left, tile_ref[t], (((1,), (1,)), ((), ())), preferred_element_type=F32
                    )
                )
            for u in range(unroll):
                acc[dst_s[i * step + g * unroll + u]] += products[u]
            return carry

        lax.fori_loop(0, step // unroll, body, 0)

        @pl.when(i == steps - 1)
        def _():
            rows = per_owner * side
            for r in range(owners):
                q = me_s[0] ^ r
                for b in range(per_owner):
                    block = acc[q * per_owner + b]
                    mean = block[:width] / block[width : width + 1]
                    outs[r][:width, b * side : (b + 1) * side] = mean.astype(BF16)
                outs[r][width:, :] = feat_ref[:, pl.ds(pl.multiple_of(q * rows, side), rows)]

    shape = (2 * width, per_owner * side)
    return pl.pallas_call(
        kernel,
        grid_spec=pltpu.PrefetchScalarGridSpec(
            num_scalar_prefetch=3,
            grid=(steps,),
            in_specs=[
                pl.BlockSpec((step, side, side), lambda i, *_: (i, 0, 0)),
                pl.BlockSpec((width, nodes), lambda i, *_: (0, 0)),
            ],
            out_specs=[pl.BlockSpec(shape, lambda i, *_: (0, 0))] * owners,
            scratch_shapes=[pltpu.VMEM((blocks, width + 16, side), F32)],
        ),
        out_shape=[jax.ShapeDtypeStruct(shape, BF16)] * owners,
        compiler_params=BIG,
        name="first_layer",
    )(dst_ids, src_ids, me, tiles, features_t)


def hidden_layer(parts, weights, bias):
    count = len(parts)
    rows = parts[0].shape[1]
    width = weights[0].shape[1]

    def kernel(*refs):
        b_ref, pre_ref, hidden_ref = refs[2 * count :]
        pre = jnp.zeros((rows, width), F32)
        for r in range(count):
            pre = pre + lax.dot_general(
                refs[r][...], refs[count + r][...], (((0,), (0,)), ((), ())),
                preferred_element_type=F32,
            )
        pre = pre + b_ref[...]
        pre_ref[...] = pre
        hidden_ref[...] = jnp.maximum(pre, 0.0).astype(BF16)

    return pl.pallas_call(
        kernel,
        in_specs=[VMEM] * (2 * count + 1),
        out_specs=[VMEM] * 2,
        out_shape=[
            jax.ShapeDtypeStruct((rows, width), F32),
            jax.ShapeDtypeStruct((rows, width), BF16),
        ],
        compiler_params=BIG,
        name="hidden_layer",
    )(*parts, *weights, bias)


def row_weights(tiles, dst_ids, blocks):
    total, side, _ = tiles.shape
    step = group_of(total, 32)
    unroll = group_of(step, 8)
    steps = total // step

    def kernel(dst_s, tile_ref, out_ref, acc):
        i = pl.program_id(0)

        @pl.when(i == 0)
        def _():
            acc[...] = jnp.zeros_like(acc)

        def body(g, carry):
            for u in range(unroll):
                t = g * unroll + u
                acc[dst_s[i * step + t]] += tile_ref[t].astype(F32)
            return carry

        lax.fori_loop(0, step // unroll, body, 0)

        @pl.when(i == steps - 1)
        def _():
            for b in range(blocks):
                out_ref[b] = jnp.broadcast_to(
                    jnp.sum(acc[b], axis=1, keepdims=True), (side, side)
                )

    return pl.pallas_call(
        kernel,
        grid_spec=pltpu.PrefetchScalarGridSpec(
            num_scalar_prefetch=1,
            grid=(steps,),
            in_specs=[pl.BlockSpec((step, side, side), lambda i, *_: (i, 0, 0))],
            out_specs=pl.BlockSpec((blocks, side, side), lambda i, *_: (0, 0, 0)),
            scratch_shapes=[pltpu.VMEM((blocks, side, side), F32)],
        ),
        out_shape=jax.ShapeDtypeStruct((blocks, side, side), F32),
        compiler_params=BIG,
        cost_estimate=pl.CostEstimate(
            flops=2 * total * side * side, bytes_accessed=2 * total * side * side, transcendentals=0
        ),
        name="row_weights",
    )(dst_ids, tiles)


def output_layer(
    tiles, dst_ids, src_ids, place, me, pools, weight, hidden, w_self, w_neigh, bias, labels,
    scale, n_feat,
):
    total, side, _ = tiles.shape
    blocks = weight.shape[0]
    width = hidden.shape[1]
    count = len(pools)
    per_pool = pools[0].shape[0]
    unit = 8 * n_feat
    share = -(-(2 * width + 8) // unit) * 8
    half = n_feat // 2
    classes = w_self.shape[1]
    step = group_of(total, 32)
    unroll = group_of(step, 32)
    steps = total // step
    lead = (((0,), (0,)), ((), ()))
    last = (((1,), (1,)), ((), ()))

    def kernel(
        dst_s, src_s, place_s, me_s, tile_ref, weight_ref, hidden_ref, ws_ref, wn_ref, bias_ref,
        labels_ref, *refs,
    ):
        pool_refs = refs[:count]
        even_ref, odd_ref, gnum_ref, own_ref, acc, pool_ref, sums, sems = refs[count:]
        i = pl.program_id(0)

        @pl.when(i == 0)
        def _():
            copies = [
                pltpu.make_async_copy(
                    pool_refs[j], pool_ref.at[pl.ds(j * per_pool, per_pool)], sems.at[j]
                )
                for j in range(count)
            ]
            for copy in copies:
                copy.start()
            acc[...] = jnp.zeros_like(acc)
            sums[...] = jnp.zeros_like(sums)
            for copy in copies:
                copy.wait()

        def body(g, carry):
            products = []
            for u in range(unroll):
                t = g * unroll + u
                products.append(
                    jnp.dot(
                        tile_ref[t],
                        pool_ref[place_s[src_s[i * step + t]]],
                        preferred_element_type=F32,
                    )
                )
            for u in range(unroll):
                acc[dst_s[i * step + g * unroll + u]] += products[u]
            return carry

        lax.fori_loop(0, step // unroll, body, 0)

        @pl.when(i == steps - 1)
        def _():
            gws = jnp.zeros((width, classes), F32)
            gwn = jnp.zeros((width, classes), F32)
            gb = jnp.zeros((1, classes), F32)
            for b in range(blocks):
                rows = slice(b * side, (b + 1) * side)
                under = weight_ref[b][:, :1]
                mean = (acc[b] / under).astype(BF16)
                own = hidden_ref[rows, :]
                logits = (
                    jnp.dot(own, ws_ref[...], preferred_element_type=F32)
                    + jnp.dot(mean, wn_ref[...], preferred_element_type=F32)
                    + bias_ref[...]
                )
                expo = jnp.exp(logits - jnp.max(logits, axis=1, keepdims=True))
                prob = expo / jnp.sum(expo, axis=1, keepdims=True)
                lane = lax.broadcasted_iota(jnp.int32, (side, classes), 1)
                onehot = jnp.where(labels_ref[rows, :] == lane, 1.0, 0.0)
                grad = (prob - onehot) * scale
                glog = grad.astype(BF16)
                gb = gb + jnp.sum(grad, axis=0, keepdims=True)
                gws = gws + lax.dot_general(own, glog, lead, preferred_element_type=F32)
                gwn = gwn + lax.dot_general(mean, glog, lead, preferred_element_type=F32)
                back = lax.dot_general(glog, wn_ref[...], last, preferred_element_type=F32)
                gnum_ref[b] = (back / under).astype(BF16)
                own_ref[rows, :] = lax.dot_general(
                    glog, ws_ref[...], last, preferred_element_type=F32
                )
            sums[:width, :] = gws
            sums[width : 2 * width, :] = gwn
            sums[2 * width : 2 * width + 8, :] = jnp.broadcast_to(gb, (8, classes))
            for r in range(n_feat):
                start = pl.multiple_of((me_s[0] ^ r) * share, 8)
                target = odd_ref if r % 2 else even_ref
                target[r // 2] = sums[pl.ds(start, share), :]

    def whole(*shape):
        return pl.BlockSpec(shape, lambda i, *_: (0,) * len(shape))

    rows = blocks * side
    out = [
        ((half, share, classes), F32),
        ((half, share, classes), F32),
        ((blocks, side, width), BF16),
        ((rows, width), F32),
    ]
    return pl.pallas_call(
        kernel,
        grid_spec=pltpu.PrefetchScalarGridSpec(
            num_scalar_prefetch=4,
            grid=(steps,),
            in_specs=[
                pl.BlockSpec((step, side, side), lambda i, *_: (i, 0, 0)),
                whole(blocks, side, side),
                whole(rows, width),
                whole(width, classes),
                whole(width, classes),
                whole(1, classes),
                whole(rows, 1),
            ]
            + [pl.BlockSpec(memory_space=pl.ANY)] * count,
            out_specs=[whole(*s) for s, _ in out],
            scratch_shapes=[
                pltpu.VMEM((blocks, side, width), F32),
                pltpu.VMEM((count * per_pool, side, width), BF16),
                pltpu.VMEM((n_feat * share, classes), F32),
                pltpu.SemaphoreType.DMA((count,)),
            ],
        ),
        out_shape=[jax.ShapeDtypeStruct(s, d) for s, d in out],
        compiler_params=BIG,
        name="output_layer",
    )(
        dst_ids, src_ids, place, me, tiles, weight, hidden, w_self, w_neigh,
        bias.reshape(1, classes), labels.reshape(rows, 1), *pools,
    )


def slot_gradients(tiles, dst_ids, src_ids, owners, mine, gnum, arrays):
    total, side, _ = tiles.shape
    blocks, _, width = gnum.shape
    slots = mine.shape[0]
    devices = owners.shape[0]
    each = slots // devices
    plane = devices // arrays
    step = group_of(total, 32)
    unroll = group_of(step, 32)
    steps = total // step

    def kernel(dst_s, src_s, owner_s, mine_s, tile_ref, gnum_ref, *refs):
        outs = refs[:arrays]
        acc, stage, sems = refs[arrays:]
        i = pl.program_id(0)

        @pl.when(i == 0)
        def _():
            acc[...] = jnp.zeros_like(acc)

        def body(g, carry):
            products = []
            for u in range(unroll):
                t = g * unroll + u
                products.append(
                    lax.dot_general(
                        tile_ref[t], gnum_ref[dst_s[i * step + t]],
                        (((0,), (0,)), ((), ())), preferred_element_type=F32,
                    )
                )
            for u in range(unroll):
                acc[src_s[i * step + g * unroll + u]] += products[u]
            return carry

        lax.fori_loop(0, step // unroll, body, 0)

        @pl.when(i == steps - 1)
        def _():
            copies = [
                pltpu.make_async_copy(stage.at[a % 2], outs[a], sems.at[a]) for a in range(arrays)
            ]
            for a in range(arrays):
                if a >= 2:
                    copies[a - 2].wait()

                def place(p, carry, a=a):
                    first = owner_s[a * plane + p] * each
                    for b in range(blocks):
                        stage[a % 2, p * blocks + b] = jnp.zeros((side, width), BF16)
                    for c in range(each):
                        target = p * blocks + mine_s[first + c]
                        stage[a % 2, target] = acc[first + c].astype(BF16)
                    return carry

                lax.fori_loop(0, plane, place, 0)
                copies[a].start()
            for a in range(max(arrays - 2, 0), arrays):
                copies[a].wait()

    shape = (plane * blocks, side, width)
    return pl.pallas_call(
        kernel,
        grid_spec=pltpu.PrefetchScalarGridSpec(
            num_scalar_prefetch=4,
            grid=(steps,),
            in_specs=[
                pl.BlockSpec((step, side, side), lambda i, *_: (i, 0, 0)),
                pl.BlockSpec(gnum.shape, lambda i, *_: (0, 0, 0)),
            ],
            out_specs=[pl.BlockSpec(memory_space=pl.ANY)] * arrays,
            scratch_shapes=[
                pltpu.VMEM((slots, side, width), F32),
                pltpu.VMEM((2,) + shape, BF16),
                pltpu.SemaphoreType.DMA((arrays,)),
            ],
        ),
        out_shape=[jax.ShapeDtypeStruct(shape, BF16)] * arrays,
        compiler_params=BIG,
        name="slot_gradients",
    )(dst_ids, src_ids, owners, mine, tiles, gnum)


def first_gradients(returned, own, pre, parts):
    terms = len(returned)
    rows, width = own.shape
    count = len(parts)
    features = parts[0].shape[0]

    def kernel(*refs):
        own_ref, pre_ref = refs[terms : terms + 2]
        part_refs = refs[terms + 2 : terms + 2 + count]
        even_ref, odd_ref = refs[terms + 2 + count :]
        grad = refs[0][...].astype(F32)
        for term in range(1, terms):
            grad = grad + refs[term][...].astype(F32)
        grad = grad + own_ref[...]
        grad_pre = jnp.where(pre_ref[...] > 0.0, grad, 0.0).astype(BF16)
        gb = jnp.sum(grad_pre.astype(F32), axis=0, keepdims=True)
        for r in range(count):
            target = odd_ref if r % 2 else even_ref
            target[r // 2, :features] = jnp.dot(
                part_refs[r][...], grad_pre, preferred_element_type=F32
            )
            target[r // 2, features:] = jnp.broadcast_to(gb, (8, width))

    shape = (count // 2, features + 8, width)
    return pl.pallas_call(
        kernel,
        in_specs=[VMEM] * (terms + 2 + count),
        out_specs=[VMEM] * 2,
        out_shape=[jax.ShapeDtypeStruct(shape, F32)] * 2,
        compiler_params=BIG,
        name="first_gradients",
    )(*returned, own, pre, *parts)


def swap(value, axis, mask):
    return lax.ppermute(value, axis, [(k, k ^ mask) for k in range(lax.axis_size(axis))])


def feat_sum(even, odd):
    value = even + swap(odd, "feat", 1)
    mask = 2
    while value.shape[0] > 1:
        value = value[0::2] + swap(value[1::2], "feat", mask)
        mask *= 2
    return value[0]


def gather_blocks(value, planes, across, beside):
    n_dom = lax.axis_size("dom")
    down = lax.axis_size("feat") // 2
    held = []
    shifted = [value] + [swap(value, "dom", across * k) for k in range(1, planes)]
    for k, own in enumerate(shifted):
        if k > 0:
            own, beside = lax.optimization_barrier((own, beside))
        aside = [own] + [swap(own, "dom", i) for i in range(1, across)]
        below = [own] + [swap(own, "feat", 2 * j) for j in range(1, down)]
        pieces = list(aside)
        for j in range(1, down):
            pieces.append(below[j])
            for i in range(1, across):
                if k % 2 == 0:
                    pieces.append(swap(aside[i], "feat", 2 * j))
                else:
                    pieces.append(swap(below[j], "dom", i))
        held.append(jnp.concatenate(pieces))
    return held + [swap(piece, "feat", 1) for piece in held]


def total_of(values):
    total = values[0].astype(F32)
    for value in values[1:]:
        total = total + value.astype(F32)
    return total.astype(BF16)


def return_blocks(arrays, planes, across):
    down = lax.axis_size("feat") // 2
    size = arrays[0].shape[0] // (across * down)
    width = arrays[0].shape[-1]
    terms = []
    for k in list(range(1, planes)) + [0]:
        other = swap(arrays[planes + k], "feat", 1)
        pair = {}
        for j in reversed(range(down)):
            for i in reversed(range(across)):
                at = slice((j * across + i) * size, (j * across + i + 1) * size)
                pair[i, j] = total_of([arrays[k][at], other[at]]).reshape(-1, width)
        parts = [pair[0, 0]]
        for i in range(1, across):
            piece = [pair[i, 0]]
            if k % 2 == 0:
                piece += [swap(pair[i, j], "feat", 2 * j) for j in range(1, down)]
            parts.append(swap(total_of(piece), "dom", i))
        for j in range(1, down):
            piece = [pair[0, j]]
            if k % 2 == 1:
                piece += [swap(pair[i, j], "dom", i) for i in range(1, across)]
            parts.append(swap(total_of(piece), "feat", 2 * j))
        if k > 0:
            parts = [swap(total_of(parts), "dom", across * k)]
        terms += parts
    return terms


def doubling_sum(value, axis):
    size = lax.axis_size(axis)
    reach = 1
    while reach < size:
        value = value + swap(value, axis, reach)
        reach *= 2
    return value


def on_device(
    inputs_t, tiles_first, first_dst, first_src, w1_self, w1_neigh, bias_first, fetch_ids,
    tiles_out, out_dst, out_src, output_self_weight, output_neighbour_weight, bias_out, labels,
):
    every = ("dom", "feat")
    n_feat = lax.axis_size("feat")
    devices = lax.axis_size("dom") * n_feat
    side = tiles_out.shape[1]
    rows_dev = labels.shape[0]
    blocks = rows_dev // side
    slots_peer = fetch_ids.shape[2]
    features, width = w1_self.shape
    classes = output_self_weight.shape[1]
    scale = 1.0 / math.sqrt(devices * rows_dev)

    me_dom, me_feat = lax.axis_index("dom"), lax.axis_index("feat")
    me = me_feat.astype(jnp.int32).reshape(1)
    planes = math.gcd(lax.axis_size("dom"), 4)
    across = lax.axis_size("dom") // planes

    mine = lax.all_to_all(fetch_ids[:, 0, :], every, split_axis=0, concat_axis=0, tiled=True)
    weights = jnp.concatenate([w1_neigh, w1_self])
    weights = [weights] + [swap(weights, "feat", r) for r in range(1, n_feat)]
    parts = first_layer(inputs_t, tiles_first, first_dst, first_src, me, n_feat * blocks, n_feat)
    parts = [parts[0]] + [swap(parts[r], "feat", r) for r in range(1, n_feat)]
    weights[0], mine = lax.optimization_barrier((weights[0], mine))
    pre, hidden = hidden_layer(parts, weights, bias_first.reshape(1, width))
    weight = row_weights(tiles_out, out_dst, blocks)
    pools = gather_blocks(hidden, planes, across, weight)
    pools = [pool.reshape(-1, side, width) for pool in pools]
    owner = jnp.arange(devices, dtype=jnp.int32)[:, None]
    off_dom = (owner // n_feat) ^ me_dom
    off_feat = (owner % n_feat) ^ me_feat
    place = (off_feat % 2) * planes + off_dom // across
    place = (place * (n_feat // 2) + off_feat // 2) * across + off_dom % across
    place = (place * blocks + mine).reshape(-1)
    even, odd, gnum, own = output_layer(
        tiles_out, out_dst, out_src, place, me, pools, weight, hidden, output_self_weight,
        output_neighbour_weight, bias_out, labels, scale, n_feat,
    )
    third = doubling_sum(feat_sum(even, odd), "dom")
    third = jnp.stack([third] + [swap(third, "feat", r) for r in range(1, n_feat)])
    third = jnp.take(third, jnp.arange(n_feat) ^ me_feat, axis=0).reshape(-1, classes)
    index = jnp.arange(devices, dtype=jnp.int32)
    plane = devices // (2 * planes)
    to_dom = me_dom ^ (index // plane % planes * across + index % across)
    to_feat = me_feat ^ (index % plane // across * 2 + index // (plane * planes))
    owners = (to_dom * n_feat + to_feat).astype(jnp.int32)
    arrays = slot_gradients(
        tiles_out, out_dst, out_src, owners, mine.reshape(-1), gnum, 2 * planes
    )
    terms = return_blocks(arrays, planes, across)
    even, odd = first_gradients(terms, own, pre, parts)
    last = doubling_sum(feat_sum(even, odd), "dom")
    edge = 2 * features
    return (
        last[features:edge],
        last[:features],
        last[edge],
        third[:width],
        third[width : 2 * width],
        third[2 * width],
    )


def solution(mesh):
    in_specs = (
        P("feat", "dom"),
        P("dom", None, None),
        P("dom"),
        P("dom"),
        P("feat", None),
        P("feat", None),
        P(),
        P(None, ("dom", "feat"), None),
        P(("dom", "feat"), None, None),
        P(("dom", "feat")),
        P(("dom", "feat")),
        P(),
        P(),
        P(),
        P(("dom", "feat")),
    )
    out_specs = (P("feat", None), P("feat", None), P(), P(), P(), P())
    return jax.shard_map(
        on_device, mesh=mesh, in_specs=in_specs, out_specs=out_specs, check_vma=False
    )
```

```python
import functools
import math

import jax
import jax.numpy as jnp
from jax import lax
from jax.experimental import pallas as pl
from jax.experimental.pallas import tpu as pltpu
from jax.sharding import PartitionSpec as P

F32 = jnp.float32
BF16 = jnp.bfloat16
BIG = pltpu.CompilerParams(vmem_limit_bytes=58 << 20)
VMEM = pl.BlockSpec(memory_space=pltpu.VMEM)


def group_of(count, most):
    return math.gcd(count, most)


def products_cost(total, side, width):
    return pl.CostEstimate(
        flops=8 * total * side * side * width,
        bytes_accessed=2 * total * side * side,
        transcendentals=0,
    )


def first_layer(features_t, tiles, dst_ids, src_ids, me, blocks, owners):
    width, nodes = features_t.shape
    total, side, _ = tiles.shape
    step = group_of(total, 32)
    unroll = group_of(step, 16)
    steps = total // step
    per_owner = blocks // owners

    def kernel(dst_s, src_s, me_s, tile_ref, feat_ref, *refs):
        outs, acc = refs[:-1], refs[-1]
        i = pl.program_id(0)

        @pl.when(i == 0)
        def _():
            acc[...] = jnp.zeros_like(acc)

        ones = jnp.ones((16, side), BF16)

        def body(g, carry):
            products = []
            for u in range(unroll):
                t = g * unroll + u
                start = pl.multiple_of(src_s[i * step + t] * side, side)
                left = jnp.concatenate([feat_ref[:, pl.ds(start, side)], ones], axis=0)
                products.append(
                    lax.dot_general(
                        left, tile_ref[t], (((1,), (1,)), ((), ())), preferred_element_type=F32
                    )
                )
            for u in range(unroll):
                acc[dst_s[i * step + g * unroll + u]] += products[u]
            return carry

        lax.fori_loop(0, step // unroll, body, 0)

        @pl.when(i == steps - 1)
        def _():
            rows = per_owner * side
            for r in range(owners):
                q = me_s[0] ^ r
                for b in range(per_owner):
                    block = acc[q * per_owner + b]
                    mean = block[:width] / block[width : width + 1]
                    outs[r][:width, b * side : (b + 1) * side] = mean.astype(BF16)
                outs[r][width:, :] = feat_ref[:, pl.ds(pl.multiple_of(q * rows, side), rows)]

    shape = (2 * width, per_owner * side)
    return pl.pallas_call(
        kernel,
        grid_spec=pltpu.PrefetchScalarGridSpec(
            num_scalar_prefetch=3,
            grid=(steps,),
            in_specs=[
                pl.BlockSpec((step, side, side), lambda i, *_: (i, 0, 0)),
                pl.BlockSpec((width, nodes), lambda i, *_: (0, 0)),
            ],
            out_specs=[pl.BlockSpec(shape, lambda i, *_: (0, 0))] * owners,
            scratch_shapes=[pltpu.VMEM((blocks, width + 16, side), F32)],
        ),
        out_shape=[jax.ShapeDtypeStruct(shape, BF16)] * owners,
        compiler_params=BIG,
        name="first_layer",
    )(dst_ids, src_ids, me, tiles, features_t)


def hidden_layer(parts, weights, bias):
    count = len(parts)
    features, rows = parts[0].shape
    width = weights[0].shape[1]

    def kernel(*refs):
        b_ref, pre_ref, hidden_ref = refs[2 * count :]
        pre = jnp.zeros((rows, width), F32)
        for r in range(count):
            pre = pre + lax.dot_general(
                refs[r][...], refs[count + r][:features, :], (((0,), (0,)), ((), ())),
                preferred_element_type=F32,
            )
        pre = pre + b_ref[...]
        pre_ref[...] = pre
        hidden_ref[:rows, :] = jnp.maximum(pre, 0.0).astype(BF16)
        row = lax.broadcasted_iota(jnp.int32, (16, width), 0)
        lists = jnp.zeros((16, width), F32)
        for r in range(count):
            one = refs[count + r][features:, :].astype(F32)[:1]
            lists = jnp.where(row == r, one, lists)
        hidden_ref[rows:, :] = lists.astype(BF16)

    return pl.pallas_call(
        kernel,
        in_specs=[VMEM] * (2 * count + 1),
        out_specs=[VMEM] * 2,
        out_shape=[
            jax.ShapeDtypeStruct((rows, width), F32),
            jax.ShapeDtypeStruct((rows + 16, width), BF16),
        ],
        compiler_params=BIG,
        name="hidden_layer",
    )(*parts, *weights, bias)


def row_weights(tiles, dst_ids, blocks):
    total, side, _ = tiles.shape
    step = group_of(total, 32)
    unroll = group_of(step, 8)
    steps = total // step

    def kernel(dst_s, tile_ref, out_ref, acc):
        i = pl.program_id(0)

        @pl.when(i == 0)
        def _():
            acc[...] = jnp.zeros_like(acc)

        def body(g, carry):
            for u in range(unroll):
                t = g * unroll + u
                acc[dst_s[i * step + t]] += tile_ref[t].astype(F32)
            return carry

        lax.fori_loop(0, step // unroll, body, 0)

        @pl.when(i == steps - 1)
        def _():
            for b in range(blocks):
                out_ref[b] = jnp.broadcast_to(
                    jnp.sum(acc[b], axis=1, keepdims=True), (side, side)
                )

    return pl.pallas_call(
        kernel,
        grid_spec=pltpu.PrefetchScalarGridSpec(
            num_scalar_prefetch=1,
            grid=(steps,),
            in_specs=[pl.BlockSpec((step, side, side), lambda i, *_: (i, 0, 0))],
            out_specs=pl.BlockSpec((blocks, side, side), lambda i, *_: (0, 0, 0)),
            scratch_shapes=[pltpu.VMEM((blocks, side, side), F32)],
        ),
        out_shape=jax.ShapeDtypeStruct((blocks, side, side), F32),
        compiler_params=BIG,
        cost_estimate=pl.CostEstimate(
            flops=2 * total * side * side, bytes_accessed=2 * total * side * side, transcendentals=0
        ),
        name="row_weights",
    )(dst_ids, tiles)


def output_layer(
    tiles, dst_ids, src_ids, place, me, pools, weight, hidden, w_self, w_neigh, bias, labels,
    scale, n_feat,
):
    total, side, _ = tiles.shape
    blocks = weight.shape[0]
    width = hidden.shape[1]
    count = len(pools)
    per_pool = pools[0].shape[0]
    classes = w_self.shape[0]
    second = -(-classes // 8) * 8
    share = -(-(2 * second + 8) // (8 * n_feat)) * 8
    step = group_of(total, 32)
    unroll = group_of(step, 32)
    steps = total // step
    lead = (((0,), (0,)), ((), ()))
    last = (((1,), (1,)), ((), ()))

    def kernel(
        dst_s, src_s, place_s, me_s, tile_ref, weight_ref, hidden_ref, ws_ref, wn_ref, bias_ref,
        labels_ref, *refs,
    ):
        pool_refs = refs[:count]
        third_refs = refs[count : count + n_feat]
        gnum_ref, own_ref, acc, pool_ref, sums_ref, sems = refs[count + n_feat :]
        i = pl.program_id(0)

        @pl.when(i == 0)
        def _():
            copies = [
                pltpu.make_async_copy(
                    pool_refs[j], pool_ref.at[pl.ds(j * per_pool, per_pool)], sems.at[j]
                )
                for j in range(count)
            ]
            for copy in copies:
                copy.start()
            acc[...] = jnp.zeros_like(acc)
            for copy in copies:
                copy.wait()

        def body(g, carry):
            products = []
            for u in range(unroll):
                t = g * unroll + u
                products.append(
                    jnp.dot(
                        tile_ref[t],
                        pool_ref[place_s[src_s[i * step + t]]],
                        preferred_element_type=F32,
                    )
                )
            for u in range(unroll):
                acc[dst_s[i * step + g * unroll + u]] += products[u]
            return carry

        lax.fori_loop(0, step // unroll, body, 0)

        @pl.when(i == steps - 1)
        def _():
            gws = jnp.zeros((classes, width), F32)
            gwn = jnp.zeros((classes, width), F32)
            gb = jnp.zeros((1, classes), F32)
            for b in range(blocks):
                rows = slice(b * side, (b + 1) * side)
                under = weight_ref[b][:, :1]
                mean = (acc[b] / under).astype(BF16)
                own = hidden_ref[rows, :]
                logits = (
                    lax.dot_general(own, ws_ref[...], last, preferred_element_type=F32)
                    + lax.dot_general(mean, wn_ref[...], last, preferred_element_type=F32)
                    + bias_ref[...]
                )
                expo = jnp.exp(logits - jnp.max(logits, axis=1, keepdims=True))
                prob = expo / jnp.sum(expo, axis=1, keepdims=True)
                lane = lax.broadcasted_iota(jnp.int32, (side, classes), 1)
                onehot = jnp.where(labels_ref[rows, :] == lane, 1.0, 0.0)
                grad = (prob - onehot) * scale
                glog = grad.astype(BF16)
                gb = gb + jnp.sum(grad, axis=0, keepdims=True)
                gws = gws + lax.dot_general(glog, own, lead, preferred_element_type=F32)
                gwn = gwn + lax.dot_general(glog, mean, lead, preferred_element_type=F32)
                back = jnp.dot(glog, wn_ref[...], preferred_element_type=F32)
                gnum_ref[b] = (back / under).astype(BF16)
                own_ref[rows, :] = jnp.dot(glog, ws_ref[...], preferred_element_type=F32)
            sums_ref[...] = jnp.zeros_like(sums_ref)
            sums_ref[:classes, :] = gws
            sums_ref[second : second + classes, :] = gwn
            sums_ref[2 * second : 2 * second + 1, :classes] = gb
            for r in range(n_feat):
                start = pl.multiple_of((me_s[0] ^ r) * share, 8)
                third_refs[r][...] = sums_ref[pl.ds(start, share), :]

    def whole(*shape):
        return pl.BlockSpec(shape, lambda i, *_: (0,) * len(shape))

    rows = blocks * side
    out = [((share, width), F32)] * n_feat + [
        ((blocks, side, width), BF16),
        ((rows, width), F32),
    ]
    return pl.pallas_call(
        kernel,
        grid_spec=pltpu.PrefetchScalarGridSpec(
            num_scalar_prefetch=4,
            grid=(steps,),
            in_specs=[
                pl.BlockSpec((step, side, side), lambda i, *_: (i, 0, 0)),
                whole(blocks, side, side),
                whole(rows + 16, width),
                whole(classes, width),
                whole(classes, width),
                whole(1, classes),
                whole(rows, 1),
            ]
            + [pl.BlockSpec(memory_space=pl.ANY)] * count,
            out_specs=[whole(*s) for s, _ in out],
            scratch_shapes=[
                pltpu.VMEM((blocks, side, width), F32),
                pltpu.VMEM((count * per_pool, side, width), BF16),
                pltpu.VMEM((n_feat * share, width), F32),
                pltpu.SemaphoreType.DMA((count,)),
            ],
        ),
        out_shape=[jax.ShapeDtypeStruct(s, d) for s, d in out],
        compiler_params=BIG,
        cost_estimate=products_cost(total, side, width),
        name="output_layer",
    )(
        dst_ids, src_ids, place, me, tiles, weight, hidden, w_self, w_neigh,
        bias.reshape(1, classes), labels, *pools,
    )


def slot_gradients(tiles, dst_ids, src_ids, owners, mine, gnum, arrays):
    total, side, _ = tiles.shape
    blocks, _, width = gnum.shape
    slots = mine.shape[0]
    devices = owners.shape[0]
    each = slots // devices
    plane = devices // arrays
    step = group_of(total, 32)
    unroll = group_of(step, 32)
    steps = total // step

    def kernel(dst_s, src_s, owner_s, mine_s, tile_ref, gnum_ref, *refs):
        outs = refs[:arrays]
        acc, stage, sems = refs[arrays:]
        i = pl.program_id(0)

        @pl.when(i == 0)
        def _():
            acc[...] = jnp.zeros_like(acc)

        def body(g, carry):
            products = []
            for u in range(unroll):
                t = g * unroll + u
                products.append(
                    lax.dot_general(
                        tile_ref[t], gnum_ref[dst_s[i * step + t]],
                        (((0,), (0,)), ((), ())), preferred_element_type=F32,
                    )
                )
            for u in range(unroll):
                acc[src_s[i * step + g * unroll + u]] += products[u]
            return carry

        lax.fori_loop(0, step // unroll, body, 0)

        @pl.when(i == steps - 1)
        def _():
            copies = [
                pltpu.make_async_copy(stage.at[a % 2], outs[a], sems.at[a]) for a in range(arrays)
            ]
            for a in range(arrays):
                if a >= 2:
                    copies[a - 2].wait()

                def place(p, carry, a=a):
                    first = owner_s[a * plane + p] * each
                    for b in range(blocks):
                        stage[a % 2, p * blocks + b] = jnp.zeros((side, width), BF16)
                    for c in range(each):
                        target = p * blocks + mine_s[first + c]
                        stage[a % 2, target] = acc[first + c].astype(BF16)
                    return carry

                lax.fori_loop(0, plane, place, 0)
                copies[a].start()
            for a in range(max(arrays - 2, 0), arrays):
                copies[a].wait()

    shape = (plane * blocks, side, width)
    return pl.pallas_call(
        kernel,
        grid_spec=pltpu.PrefetchScalarGridSpec(
            num_scalar_prefetch=4,
            grid=(steps,),
            in_specs=[
                pl.BlockSpec((step, side, side), lambda i, *_: (i, 0, 0)),
                pl.BlockSpec(gnum.shape, lambda i, *_: (0, 0, 0)),
            ],
            out_specs=[pl.BlockSpec(memory_space=pl.ANY)] * arrays,
            scratch_shapes=[
                pltpu.VMEM((slots, side, width), F32),
                pltpu.VMEM((2,) + shape, BF16),
                pltpu.SemaphoreType.DMA((arrays,)),
            ],
        ),
        out_shape=[jax.ShapeDtypeStruct(shape, BF16)] * arrays,
        compiler_params=BIG,
        cost_estimate=products_cost(total, side, width),
        name="slot_gradients",
    )(dst_ids, src_ids, owners, mine, tiles, gnum)


def first_gradients(returned, own, pre, parts):
    terms = len(returned)
    rows, width = own.shape
    count = len(parts)
    features = parts[0].shape[0]

    def kernel(*refs):
        own_ref, pre_ref = refs[terms : terms + 2]
        part_refs = refs[terms + 2 : terms + 2 + count]
        even_ref, odd_ref = refs[terms + 2 + count :]
        grad = refs[0][...].astype(F32)
        for term in range(1, terms):
            grad = grad + refs[term][...].astype(F32)
        grad = grad + own_ref[...]
        grad_pre = jnp.where(pre_ref[...] > 0.0, grad, 0.0).astype(BF16)
        gb = jnp.sum(grad_pre.astype(F32), axis=0, keepdims=True)
        for r in range(count):
            target = odd_ref if r % 2 else even_ref
            target[r // 2, :features] = jnp.dot(
                part_refs[r][...], grad_pre, preferred_element_type=F32
            )
            target[r // 2, features:] = jnp.broadcast_to(gb, (8, width))

    shape = (count // 2, features + 8, width)
    return pl.pallas_call(
        kernel,
        in_specs=[VMEM] * (terms + 2 + count),
        out_specs=[VMEM] * 2,
        out_shape=[jax.ShapeDtypeStruct(shape, F32)] * 2,
        compiler_params=BIG,
        name="first_gradients",
    )(*returned, own, pre, *parts)


def swap(value, axis, mask):
    return lax.ppermute(value, axis, [(k, k ^ mask) for k in range(lax.axis_size(axis))])


def feat_sum(even, odd):
    value = even + swap(odd, "feat", 1)
    mask = 2
    while value.shape[0] > 1:
        value = value[0::2] + swap(value[1::2], "feat", mask)
        mask *= 2
    return value[0]


def gather_blocks(value, planes, across, rows, beside):
    n_dom = lax.axis_size("dom")
    down = lax.axis_size("feat") // 2
    held, tails = [], []
    shifted = [value] + [swap(value, "dom", across * k) for k in range(1, planes)]
    for k, own in enumerate(shifted):
        if k > 0:
            own, beside = lax.optimization_barrier((own, beside))
        aside = [own] + [swap(own, "dom", i) for i in range(1, across)]
        below = [own] + [swap(own, "feat", 2 * j) for j in range(1, down)]
        pieces = list(aside)
        for j in range(1, down):
            pieces.append(below[j])
            for i in range(1, across):
                if k % 2 == 0:
                    pieces.append(swap(aside[i], "feat", 2 * j))
                else:
                    pieces.append(swap(below[j], "dom", i))
        held.append(jnp.concatenate([piece[:rows] for piece in pieces]))
        tails += [piece[rows:] for piece in aside]
    return held + [swap(piece, "feat", 1) for piece in held], jnp.stack(tails)


def total_of(values):
    total = values[0].astype(F32)
    for value in values[1:]:
        total = total + value.astype(F32)
    return total.astype(BF16)


def return_blocks(arrays, planes, across):
    down = lax.axis_size("feat") // 2
    size = arrays[0].shape[0] // (across * down)
    width = arrays[0].shape[-1]
    terms = []
    for k in list(range(1, planes)) + [0]:
        other = swap(arrays[planes + k], "feat", 1)
        pair = {}
        for j in reversed(range(down)):
            for i in reversed(range(across)):
                at = slice((j * across + i) * size, (j * across + i + 1) * size)
                pair[i, j] = total_of([arrays[k][at], other[at]]).reshape(-1, width)
        parts = [pair[0, 0]]
        for i in range(1, across):
            piece = [pair[i, 0]]
            if k % 2 == 0:
                piece += [swap(pair[i, j], "feat", 2 * j) for j in range(1, down)]
            parts.append(swap(total_of(piece), "dom", i))
        for j in range(1, down):
            piece = [pair[0, j]]
            if k % 2 == 1:
                piece += [swap(pair[i, j], "dom", i) for i in range(1, across)]
            parts.append(swap(total_of(piece), "feat", 2 * j))
        if k > 0:
            parts = [swap(total_of(parts), "dom", across * k)]
        terms += parts
    return terms


def doubling_sum(value, axis):
    size = lax.axis_size(axis)
    reach = 1
    while reach < size:
        value = value + swap(value, axis, reach)
        reach *= 2
    return value


def on_device(
    inputs_t, tiles_first, first_dst, first_src, w1_self, w1_neigh, bias_first, fetch_ids,
    tiles_out, out_dst, out_src, output_self_weight, output_neighbour_weight, bias_out, labels,
):
    n_feat = lax.axis_size("feat")
    devices = lax.axis_size("dom") * n_feat
    side = tiles_out.shape[1]
    rows_dev = labels.shape[0]
    blocks = rows_dev // side
    slots_peer = fetch_ids.shape[2]
    features, width = w1_self.shape
    classes = output_self_weight.shape[1]
    scale = 1.0 / math.sqrt(devices * rows_dev)

    me_dom, me_feat = lax.axis_index("dom"), lax.axis_index("feat")
    me = me_feat.astype(jnp.int32).reshape(1)
    planes = math.gcd(lax.axis_size("dom"), 4)
    across = lax.axis_size("dom") // planes

    listed = jnp.pad(
        fetch_ids.reshape(1, -1).astype(BF16), ((0, 15), (0, width - devices * slots_peer))
    )
    weights = jnp.concatenate([w1_neigh, w1_self, listed])
    weights = [weights] + [swap(weights, "feat", r) for r in range(1, n_feat)]
    parts = first_layer(inputs_t, tiles_first, first_dst, first_src, me, n_feat * blocks, n_feat)
    parts = [parts[0]] + [swap(parts[r], "feat", r) for r in range(1, n_feat)]
    pre, hidden = hidden_layer(parts, weights, bias_first.reshape(1, width))
    hidden, dst = lax.optimization_barrier((hidden, out_dst))
    weight = row_weights(tiles_out, dst, blocks)
    index = jnp.arange(devices, dtype=jnp.int32)
    plane = devices // (2 * planes)
    to_dom = me_dom ^ (index // plane % planes * across + index % across)
    to_feat = me_feat ^ (index % plane // across * 2 + index // (plane * planes))
    owners = (to_dom * n_feat + to_feat).astype(jnp.int32)
    here = me_dom * n_feat + me_feat
    pools, lists = gather_blocks(hidden, planes, across, rows_dev, weight)
    pools = [pool.reshape(-1, side, width) for pool in pools]
    mine = lax.dynamic_slice_in_dim(lists[:, :n_feat], here * slots_peer, slots_peer, axis=2)
    mine = mine.reshape(devices, slots_peer).astype(jnp.int32)
    mine = jnp.take(mine, index ^ here, axis=0)
    off = index[:, None] ^ here
    place = off % 2 * planes + off // n_feat // across
    place = (place * (n_feat // 2) + off % n_feat // 2) * across + off // n_feat % across
    place = (place * blocks + mine).reshape(-1)
    mine = mine.reshape(-1)
    column = labels.reshape(rows_dev, 1)
    *third, gnum, own = output_layer(
        tiles_out, out_dst, out_src, place, me, pools, weight, hidden, output_self_weight.T,
        output_neighbour_weight.T, bias_out, column, scale, n_feat,
    )
    third = [third[0]] + [swap(third[r], "feat", r) for r in range(1, n_feat)]
    arrays = slot_gradients(
        tiles_out, out_dst, out_src, owners, mine, gnum, 2 * planes
    )
    arrays, third = lax.optimization_barrier((arrays, third))
    third = doubling_sum(functools.reduce(jnp.add, third), "dom")
    third = jnp.stack([third] + [swap(third, "feat", r) for r in range(1, n_feat)])
    third = jnp.take(third, jnp.arange(n_feat) ^ me_feat, axis=0).reshape(-1, width)
    second = -(-classes // 8) * 8
    terms = return_blocks(arrays, planes, across)
    even, odd = first_gradients(terms, own, pre, parts)
    last = doubling_sum(feat_sum(even, odd), "dom")
    edge = 2 * features
    return (
        last[features:edge],
        last[:features],
        last[edge],
        third[:classes].T,
        third[second : second + classes].T,
        third[2 * second, :classes],
    )


def solution(mesh):
    in_specs = (
        P("feat", "dom"),
        P("dom", None, None),
        P("dom"),
        P("dom"),
        P("feat", None),
        P("feat", None),
        P(),
        P(None, ("dom", "feat"), None),
        P(("dom", "feat"), None, None),
        P(("dom", "feat")),
        P(("dom", "feat")),
        P(),
        P(),
        P(),
        P(("dom", "feat")),
    )
    out_specs = (P("feat", None), P("feat", None), P(), P(), P(), P())
    return jax.shard_map(
        on_device, mesh=mesh, in_specs=in_specs, out_specs=out_specs, check_vma=False
    )
```

```python
import functools
import math

import jax
import jax.numpy as jnp
from jax import lax
from jax.experimental import pallas as pl
from jax.experimental.pallas import tpu as pltpu
from jax.sharding import PartitionSpec as P

F32 = jnp.float32
BF16 = jnp.bfloat16
BIG = pltpu.CompilerParams(vmem_limit_bytes=58 << 20)
VMEM = pl.BlockSpec(memory_space=pltpu.VMEM)


def group_of(count, most):
    return math.gcd(count, most)


def products_cost(total, side, width):
    return pl.CostEstimate(
        flops=8 * total * side * side * width,
        bytes_accessed=2 * total * side * side,
        transcendentals=0,
    )


def first_layer(features_t, tiles, dst_ids, src_ids, me, blocks, owners):
    width, nodes = features_t.shape
    total, side, _ = tiles.shape
    step = group_of(total, 32)
    unroll = group_of(step, 16)
    steps = total // step
    per_owner = blocks // owners

    def kernel(dst_s, src_s, me_s, tile_ref, feat_ref, *refs):
        outs, acc = refs[:-1], refs[-1]
        i = pl.program_id(0)

        @pl.when(i == 0)
        def _():
            acc[...] = jnp.zeros_like(acc)

        ones = jnp.ones((16, side), BF16)

        def body(g, carry):
            products = []
            for u in range(unroll):
                t = g * unroll + u
                start = pl.multiple_of(src_s[i * step + t] * side, side)
                left = jnp.concatenate([feat_ref[:, pl.ds(start, side)], ones], axis=0)
                products.append(
                    lax.dot_general(
                        left, tile_ref[t], (((1,), (1,)), ((), ())), preferred_element_type=F32
                    )
                )
            for u in range(unroll):
                acc[dst_s[i * step + g * unroll + u]] += products[u]
            return carry

        lax.fori_loop(0, step // unroll, body, 0)

        @pl.when(i == steps - 1)
        def _():
            rows = per_owner * side
            for r in range(owners):
                q = me_s[0] ^ r
                for b in range(per_owner):
                    block = acc[q * per_owner + b]
                    mean = block[:width] / block[width : width + 1]
                    outs[r][:width, b * side : (b + 1) * side] = mean.astype(BF16)
                outs[r][width:, :] = feat_ref[:, pl.ds(pl.multiple_of(q * rows, side), rows)]

    shape = (2 * width, per_owner * side)
    return pl.pallas_call(
        kernel,
        grid_spec=pltpu.PrefetchScalarGridSpec(
            num_scalar_prefetch=3,
            grid=(steps,),
            in_specs=[
                pl.BlockSpec((step, side, side), lambda i, *_: (i, 0, 0)),
                pl.BlockSpec((width, nodes), lambda i, *_: (0, 0)),
            ],
            out_specs=[pl.BlockSpec(shape, lambda i, *_: (0, 0))] * owners,
            scratch_shapes=[pltpu.VMEM((blocks, width + 16, side), F32)],
        ),
        out_shape=[jax.ShapeDtypeStruct(shape, BF16)] * owners,
        compiler_params=BIG,
        name="first_layer",
    )(dst_ids, src_ids, me, tiles, features_t)


def hidden_layer(parts, weights, bias):
    count = len(parts)
    features, rows = parts[0].shape
    width = weights[0].shape[1]

    def kernel(*refs):
        b_ref, pre_ref, hidden_ref = refs[2 * count :]
        pre = jnp.zeros((rows, width), F32)
        for r in range(count):
            pre = pre + lax.dot_general(
                refs[r][...], refs[count + r][:features, :], (((0,), (0,)), ((), ())),
                preferred_element_type=F32,
            )
        pre = pre + b_ref[...]
        pre_ref[...] = pre
        hidden_ref[:rows, :] = jnp.maximum(pre, 0.0).astype(BF16)
        row = lax.broadcasted_iota(jnp.int32, (16, width), 0)
        lists = jnp.zeros((16, width), F32)
        for r in range(count):
            one = refs[count + r][features:, :].astype(F32)[:1]
            lists = jnp.where(row == r, one, lists)
        hidden_ref[rows:, :] = lists.astype(BF16)

    return pl.pallas_call(
        kernel,
        in_specs=[VMEM] * (2 * count + 1),
        out_specs=[VMEM] * 2,
        out_shape=[
            jax.ShapeDtypeStruct((rows, width), F32),
            jax.ShapeDtypeStruct((rows + 16, width), BF16),
        ],
        compiler_params=BIG,
        name="hidden_layer",
    )(*parts, *weights, bias)


def row_weights(tiles, dst_ids, blocks):
    total, side, _ = tiles.shape
    step = group_of(total, 32)
    unroll = group_of(step, 8)
    steps = total // step

    def kernel(dst_s, tile_ref, out_ref, acc):
        i = pl.program_id(0)

        @pl.when(i == 0)
        def _():
            acc[...] = jnp.zeros_like(acc)

        def body(g, carry):
            for u in range(unroll):
                t = g * unroll + u
                acc[dst_s[i * step + t]] += tile_ref[t].astype(F32)
            return carry

        lax.fori_loop(0, step // unroll, body, 0)

        @pl.when(i == steps - 1)
        def _():
            for b in range(blocks):
                out_ref[b] = jnp.broadcast_to(
                    jnp.sum(acc[b], axis=1, keepdims=True), (side, side)
                )

    return pl.pallas_call(
        kernel,
        grid_spec=pltpu.PrefetchScalarGridSpec(
            num_scalar_prefetch=1,
            grid=(steps,),
            in_specs=[pl.BlockSpec((step, side, side), lambda i, *_: (i, 0, 0))],
            out_specs=pl.BlockSpec((blocks, side, side), lambda i, *_: (0, 0, 0)),
            scratch_shapes=[pltpu.VMEM((blocks, side, side), F32)],
        ),
        out_shape=jax.ShapeDtypeStruct((blocks, side, side), F32),
        compiler_params=BIG,
        cost_estimate=pl.CostEstimate(
            flops=2 * total * side * side, bytes_accessed=2 * total * side * side, transcendentals=0
        ),
        name="row_weights",
    )(dst_ids, tiles)


def output_layer(
    tiles, dst_ids, src_ids, place, me, pools, weight, hidden, w_self, w_neigh, bias, labels,
    scale, n_feat,
):
    total, side, _ = tiles.shape
    blocks = weight.shape[0]
    width = hidden.shape[1]
    count = len(pools)
    per_pool = pools[0].shape[0]
    classes = w_self.shape[0]
    second = -(-classes // 8) * 8
    share = -(-(2 * second + 8) // (8 * n_feat)) * 8
    step = group_of(total, 64)
    unroll = group_of(step, 64)
    steps = total // step
    lead = (((0,), (0,)), ((), ()))
    last = (((1,), (1,)), ((), ()))

    def kernel(
        dst_s, src_s, place_s, me_s, tile_ref, weight_ref, hidden_ref, ws_ref, wn_ref, bias_ref,
        labels_ref, *refs,
    ):
        pool_refs = refs[:count]
        third_refs = refs[count : count + n_feat]
        gnum_ref, own_ref, acc, pool_ref, sums_ref, sems = refs[count + n_feat :]
        i = pl.program_id(0)

        @pl.when(i == 0)
        def _():
            copies = [
                pltpu.make_async_copy(
                    pool_refs[j], pool_ref.at[pl.ds(j * per_pool, per_pool)], sems.at[j]
                )
                for j in range(count)
            ]
            for copy in copies:
                copy.start()
            acc[...] = jnp.zeros_like(acc)
            for copy in copies:
                copy.wait()

        def body(g, carry):
            products = []
            for u in range(unroll):
                t = g * unroll + u
                products.append(
                    jnp.dot(
                        tile_ref[t],
                        pool_ref[place_s[src_s[i * step + t]]],
                        preferred_element_type=F32,
                    )
                )
            for u in range(unroll):
                acc[dst_s[i * step + g * unroll + u]] += products[u]
            return carry

        lax.fori_loop(0, step // unroll, body, 0)

        @pl.when(i == steps - 1)
        def _():
            gws = jnp.zeros((classes, width), F32)
            gwn = jnp.zeros((classes, width), F32)
            gb = jnp.zeros((1, classes), F32)
            for b in range(blocks):
                rows = slice(b * side, (b + 1) * side)
                under = weight_ref[b][:, :1]
                mean = (acc[b] / under).astype(BF16)
                own = hidden_ref[rows, :]
                logits = (
                    lax.dot_general(own, ws_ref[...], last, preferred_element_type=F32)
                    + lax.dot_general(mean, wn_ref[...], last, preferred_element_type=F32)
                    + bias_ref[...]
                )
                expo = jnp.exp(logits - jnp.max(logits, axis=1, keepdims=True))
                prob = expo / jnp.sum(expo, axis=1, keepdims=True)
                lane = lax.broadcasted_iota(jnp.int32, (side, classes), 1)
                onehot = jnp.where(labels_ref[rows, :] == lane, 1.0, 0.0)
                grad = (prob - onehot) * scale
                glog = grad.astype(BF16)
                gb = gb + jnp.sum(grad, axis=0, keepdims=True)
                gws = gws + lax.dot_general(glog, own, lead, preferred_element_type=F32)
                gwn = gwn + lax.dot_general(glog, mean, lead, preferred_element_type=F32)
                back = jnp.dot(glog, wn_ref[...], preferred_element_type=F32)
                gnum_ref[b] = (back / under).astype(BF16)
                own_ref[rows, :] = jnp.dot(glog, ws_ref[...], preferred_element_type=F32)
            sums_ref[...] = jnp.zeros_like(sums_ref)
            sums_ref[:classes, :] = gws
            sums_ref[second : second + classes, :] = gwn
            sums_ref[2 * second : 2 * second + 1, :classes] = gb
            for r in range(n_feat):
                start = pl.multiple_of((me_s[0] ^ r) * share, 8)
                third_refs[r][...] = sums_ref[pl.ds(start, share), :]

    def whole(*shape):
        return pl.BlockSpec(shape, lambda i, *_: (0,) * len(shape))

    rows = blocks * side
    out = [((share, width), F32)] * n_feat + [
        ((blocks, side, width), BF16),
        ((rows, width), F32),
    ]
    return pl.pallas_call(
        kernel,
        grid_spec=pltpu.PrefetchScalarGridSpec(
            num_scalar_prefetch=4,
            grid=(steps,),
            in_specs=[
                pl.BlockSpec((step, side, side), lambda i, *_: (i, 0, 0)),
                whole(blocks, side, side),
                whole(rows + 16, width),
                whole(classes, width),
                whole(classes, width),
                whole(1, classes),
                whole(rows, 1),
            ]
            + [pl.BlockSpec(memory_space=pl.ANY)] * count,
            out_specs=[whole(*s) for s, _ in out],
            scratch_shapes=[
                pltpu.VMEM((blocks, side, width), F32),
                pltpu.VMEM((count * per_pool, side, width), BF16),
                pltpu.VMEM((n_feat * share, width), F32),
                pltpu.SemaphoreType.DMA((count,)),
            ],
        ),
        out_shape=[jax.ShapeDtypeStruct(s, d) for s, d in out],
        compiler_params=BIG,
        cost_estimate=products_cost(total, side, width),
        name="output_layer",
    )(
        dst_ids, src_ids, place, me, tiles, weight, hidden, w_self, w_neigh,
        bias.reshape(1, classes), labels, *pools,
    )


def slot_gradients(tiles, dst_ids, src_ids, owners, mine, gnum, arrays):
    total, side, _ = tiles.shape
    blocks, _, width = gnum.shape
    slots = mine.shape[0]
    devices = owners.shape[0]
    each = slots // devices
    plane = devices // arrays
    step = group_of(total, 64)
    unroll = group_of(step, 64)
    steps = total // step

    def kernel(dst_s, src_s, owner_s, mine_s, tile_ref, gnum_ref, *refs):
        outs = refs[:arrays]
        acc, stage, sems = refs[arrays:]
        i = pl.program_id(0)

        @pl.when(i == 0)
        def _():
            acc[...] = jnp.zeros_like(acc)

        def body(g, carry):
            products = []
            for u in range(unroll):
                t = g * unroll + u
                products.append(
                    lax.dot_general(
                        tile_ref[t], gnum_ref[dst_s[i * step + t]],
                        (((0,), (0,)), ((), ())), preferred_element_type=F32,
                    )
                )
            for u in range(unroll):
                acc[src_s[i * step + g * unroll + u]] += products[u]
            return carry

        lax.fori_loop(0, step // unroll, body, 0)

        @pl.when(i == steps - 1)
        def _():
            copies = [
                pltpu.make_async_copy(stage.at[a % 2], outs[a], sems.at[a]) for a in range(arrays)
            ]
            for a in range(arrays):
                if a >= 2:
                    copies[a - 2].wait()

                def place(p, carry, a=a):
                    first = owner_s[a * plane + p] * each
                    for b in range(blocks):
                        stage[a % 2, p * blocks + b] = jnp.zeros((side, width), BF16)
                    for c in range(each):
                        target = p * blocks + mine_s[first + c]
                        stage[a % 2, target] = acc[first + c].astype(BF16)
                    return carry

                lax.fori_loop(0, plane, place, 0)
                copies[a].start()
            for a in range(max(arrays - 2, 0), arrays):
                copies[a].wait()

    shape = (plane * blocks, side, width)
    return pl.pallas_call(
        kernel,
        grid_spec=pltpu.PrefetchScalarGridSpec(
            num_scalar_prefetch=4,
            grid=(steps,),
            in_specs=[
                pl.BlockSpec((step, side, side), lambda i, *_: (i, 0, 0)),
                pl.BlockSpec(gnum.shape, lambda i, *_: (0, 0, 0)),
            ],
            out_specs=[pl.BlockSpec(memory_space=pl.ANY)] * arrays,
            scratch_shapes=[
                pltpu.VMEM((slots, side, width), F32),
                pltpu.VMEM((2,) + shape, BF16),
                pltpu.SemaphoreType.DMA((arrays,)),
            ],
        ),
        out_shape=[jax.ShapeDtypeStruct(shape, BF16)] * arrays,
        compiler_params=BIG,
        cost_estimate=products_cost(total, side, width),
        name="slot_gradients",
    )(dst_ids, src_ids, owners, mine, tiles, gnum)


def first_gradients(returned, own, pre, parts):
    terms = len(returned)
    rows, width = own.shape
    count = len(parts)
    features = parts[0].shape[0]

    def kernel(*refs):
        own_ref, pre_ref = refs[terms : terms + 2]
        part_refs = refs[terms + 2 : terms + 2 + count]
        outs = refs[terms + 2 + count :]
        grad = refs[0][...].astype(F32)
        for term in range(1, terms):
            grad = grad + refs[term][...].astype(F32)
        grad = grad + own_ref[...]
        grad_pre = jnp.where(pre_ref[...] > 0.0, grad, 0.0).astype(BF16)
        gb = jnp.sum(grad_pre.astype(F32), axis=0, keepdims=True)
        for r in range(count):
            outs[r][:features] = jnp.dot(part_refs[r][...], grad_pre, preferred_element_type=F32)
            outs[r][features:] = jnp.broadcast_to(gb, (8, width))

    shape = (features + 8, width)
    return pl.pallas_call(
        kernel,
        in_specs=[VMEM] * (terms + 2 + count),
        out_specs=[VMEM] * count,
        out_shape=[jax.ShapeDtypeStruct(shape, F32)] * count,
        compiler_params=BIG,
        name="first_gradients",
    )(*returned, own, pre, *parts)


def swap(value, axis, mask):
    return lax.ppermute(value, axis, [(k, k ^ mask) for k in range(lax.axis_size(axis))])


def feat_sum(pieces):
    total = pieces[0]
    for r in range(1, len(pieces)):
        total = total + swap(pieces[r], "feat", r)
    return total


def gather_blocks(value, planes, across, rows, beside):
    n_dom = lax.axis_size("dom")
    down = lax.axis_size("feat") // 2
    held, tails = [], []
    shifted = [value] + [swap(value, "dom", across * k) for k in range(1, planes)]
    for k, own in enumerate(shifted):
        if k > 0:
            own, beside = lax.optimization_barrier((own, beside))
        aside = [own] + [swap(own, "dom", i) for i in range(1, across)]
        below = [own] + [swap(own, "feat", 2 * j) for j in range(1, down)]
        pieces = list(aside)
        for j in range(1, down):
            pieces.append(below[j])
            for i in range(1, across):
                if k % 2 == 0:
                    pieces.append(swap(aside[i], "feat", 2 * j))
                else:
                    pieces.append(swap(below[j], "dom", i))
        held.append(jnp.concatenate([piece[:rows] for piece in pieces]))
        tails += [piece[rows:] for piece in aside]
    return held + [swap(piece, "feat", 1) for piece in held], jnp.stack(tails)


def total_of(values):
    total = values[0].astype(F32)
    for value in values[1:]:
        total = total + value.astype(F32)
    return total.astype(BF16)


def return_blocks(arrays, planes, across):
    down = lax.axis_size("feat") // 2
    size = arrays[0].shape[0] // (across * down)
    width = arrays[0].shape[-1]
    terms = []
    for k in list(range(1, planes)) + [0]:
        other = swap(arrays[planes + k], "feat", 1)
        pair = {}
        for j in reversed(range(down)):
            for i in reversed(range(across)):
                at = slice((j * across + i) * size, (j * across + i + 1) * size)
                pair[i, j] = total_of([arrays[k][at], other[at]]).reshape(-1, width)
        parts = [pair[0, 0]]
        for i in range(1, across):
            piece = [pair[i, 0]]
            if k % 2 == 0:
                piece += [swap(pair[i, j], "feat", 2 * j) for j in range(1, down)]
            parts.append(swap(total_of(piece), "dom", i))
        for j in range(1, down):
            piece = [pair[0, j]]
            if k % 2 == 1:
                piece += [swap(pair[i, j], "dom", i) for i in range(1, across)]
            parts.append(swap(total_of(piece), "feat", 2 * j))
        if k > 0:
            parts = [swap(total_of(parts), "dom", across * k)]
        terms += parts
    return terms


def doubling_sum(value, axis):
    size = lax.axis_size(axis)
    reach = 1
    while reach < size:
        value = value + swap(value, axis, reach)
        reach *= 2
    return value


def on_device(
    inputs_t, tiles_first, first_dst, first_src, w1_self, w1_neigh, bias_first, fetch_ids,
    tiles_out, out_dst, out_src, output_self_weight, output_neighbour_weight, bias_out, labels,
):
    n_feat = lax.axis_size("feat")
    devices = lax.axis_size("dom") * n_feat
    side = tiles_out.shape[1]
    rows_dev = labels.shape[0]
    blocks = rows_dev // side
    slots_peer = fetch_ids.shape[2]
    features, width = w1_self.shape
    classes = output_self_weight.shape[1]
    scale = 1.0 / math.sqrt(devices * rows_dev)

    me_dom, me_feat = lax.axis_index("dom"), lax.axis_index("feat")
    me = me_feat.astype(jnp.int32).reshape(1)
    planes = math.gcd(lax.axis_size("dom"), 4)
    across = lax.axis_size("dom") // planes

    listed = jnp.pad(
        fetch_ids.reshape(1, -1).astype(BF16), ((0, 15), (0, width - devices * slots_peer))
    )
    weights = jnp.concatenate([w1_neigh, w1_self, listed])
    weights = [weights] + [swap(weights, "feat", r) for r in range(1, n_feat)]
    parts = first_layer(inputs_t, tiles_first, first_dst, first_src, me, n_feat * blocks, n_feat)
    parts = [parts[0]] + [swap(parts[r], "feat", r) for r in range(1, n_feat)]
    pre, hidden = hidden_layer(parts, weights, bias_first.reshape(1, width))
    hidden, dst = lax.optimization_barrier((hidden, out_dst))
    weight = row_weights(tiles_out, dst, blocks)
    index = jnp.arange(devices, dtype=jnp.int32)
    plane = devices // (2 * planes)
    to_dom = me_dom ^ (index // plane % planes * across + index % across)
    to_feat = me_feat ^ (index % plane // across * 2 + index // (plane * planes))
    owners = (to_dom * n_feat + to_feat).astype(jnp.int32)
    here = me_dom * n_feat + me_feat
    pools, lists = gather_blocks(hidden, planes, across, rows_dev, weight)
    pools = [pool.reshape(-1, side, width) for pool in pools]
    mine = lax.dynamic_slice_in_dim(lists[:, :n_feat], here * slots_peer, slots_peer, axis=2)
    mine = mine.reshape(devices, slots_peer).astype(jnp.int32)
    mine = jnp.take(mine, index ^ here, axis=0)
    off = index[:, None] ^ here
    place = off % 2 * planes + off // n_feat // across
    place = (place * (n_feat // 2) + off % n_feat // 2) * across + off // n_feat % across
    place = (place * blocks + mine).reshape(-1)
    mine = mine.reshape(-1)
    column = labels.reshape(rows_dev, 1)
    *third, gnum, own = output_layer(
        tiles_out, out_dst, out_src, place, me, pools, weight, hidden, output_self_weight.T,
        output_neighbour_weight.T, bias_out, column, scale, n_feat,
    )
    third = [third[0]] + [swap(third[r], "feat", r) for r in range(1, n_feat)]
    arrays = slot_gradients(
        tiles_out, out_dst, out_src, owners, mine, gnum, 2 * planes
    )
    arrays, third = lax.optimization_barrier((arrays, third))
    third = doubling_sum(functools.reduce(jnp.add, third), "dom")
    third = jnp.stack([third] + [swap(third, "feat", r) for r in range(1, n_feat)])
    third = jnp.take(third, jnp.arange(n_feat) ^ me_feat, axis=0).reshape(-1, width)
    second = -(-classes // 8) * 8
    terms = return_blocks(arrays, planes, across)
    pieces = first_gradients(terms, own, pre, parts)
    last = doubling_sum(feat_sum(pieces), "dom")
    edge = 2 * features
    return (
        last[features:edge],
        last[:features],
        last[edge],
        third[:classes].T,
        third[second : second + classes].T,
        third[2 * second, :classes],
    )


def solution(mesh):
    in_specs = (
        P("feat", "dom"),
        P("dom", None, None),
        P("dom"),
        P("dom"),
        P("feat", None),
        P("feat", None),
        P(),
        P(None, ("dom", "feat"), None),
        P(("dom", "feat"), None, None),
        P(("dom", "feat")),
        P(("dom", "feat")),
        P(),
        P(),
        P(),
        P(("dom", "feat")),
    )
    out_specs = (P("feat", None), P("feat", None), P(), P(), P(), P())
    return jax.shard_map(
        on_device, mesh=mesh, in_specs=in_specs, out_specs=out_specs, check_vma=False
    )
```

```python
import functools
import math

import jax
import jax.numpy as jnp
from jax import lax
from jax.experimental import pallas as pl
from jax.experimental.pallas import tpu as pltpu
from jax.sharding import PartitionSpec as P

F32 = jnp.float32
BF16 = jnp.bfloat16
BIG = pltpu.CompilerParams(vmem_limit_bytes=58 << 20)
VMEM = pl.BlockSpec(memory_space=pltpu.VMEM)


def group_of(count, most):
    return math.gcd(count, most)


def products_cost(total, side, width):
    return pl.CostEstimate(
        flops=8 * total * side * side * width,
        bytes_accessed=2 * total * side * side,
        transcendentals=0,
    )


def first_layer(features_t, tiles, dst_ids, src_ids, me, blocks, owners):
    width, nodes = features_t.shape
    total, side, _ = tiles.shape
    step = group_of(total, 32)
    unroll = group_of(step, 16)
    steps = total // step
    per_owner = blocks // owners

    def kernel(dst_s, src_s, me_s, tile_ref, feat_ref, *refs):
        outs, acc = refs[:-1], refs[-1]
        i = pl.program_id(0)

        @pl.when(i == 0)
        def _():
            acc[...] = jnp.zeros_like(acc)

        ones = jnp.ones((16, side), BF16)

        def body(g, carry):
            products = []
            for u in range(unroll):
                t = g * unroll + u
                start = pl.multiple_of(src_s[i * step + t] * side, side)
                left = jnp.concatenate([feat_ref[:, pl.ds(start, side)], ones], axis=0)
                products.append(
                    lax.dot_general(
                        left, tile_ref[t], (((1,), (1,)), ((), ())), preferred_element_type=F32
                    )
                )
            for u in range(unroll):
                acc[dst_s[i * step + g * unroll + u]] += products[u]
            return carry

        lax.fori_loop(0, step // unroll, body, 0)

        @pl.when(i == steps - 1)
        def _():
            rows = per_owner * side
            for r in range(owners):
                q = me_s[0] ^ r
                for b in range(per_owner):
                    block = acc[q * per_owner + b]
                    mean = block[:width] / block[width : width + 1]
                    outs[r][:width, b * side : (b + 1) * side] = mean.astype(BF16)
                outs[r][width:, :] = feat_ref[:, pl.ds(pl.multiple_of(q * rows, side), rows)]

    shape = (2 * width, per_owner * side)
    return pl.pallas_call(
        kernel,
        grid_spec=pltpu.PrefetchScalarGridSpec(
            num_scalar_prefetch=3,
            grid=(steps,),
            in_specs=[
                pl.BlockSpec((step, side, side), lambda i, *_: (i, 0, 0)),
                pl.BlockSpec((width, nodes), lambda i, *_: (0, 0)),
            ],
            out_specs=[pl.BlockSpec(shape, lambda i, *_: (0, 0))] * owners,
            scratch_shapes=[pltpu.VMEM((blocks, width + 16, side), F32)],
        ),
        out_shape=[jax.ShapeDtypeStruct(shape, BF16)] * owners,
        compiler_params=BIG,
        name="first_layer",
    )(dst_ids, src_ids, me, tiles, features_t)


def hidden_layer(parts, weights, bias):
    count = len(parts)
    features, rows = parts[0].shape
    width = weights[0].shape[1]

    def kernel(*refs):
        b_ref, pre_ref, hidden_ref = refs[2 * count :]
        pre = jnp.zeros((rows, width), F32)
        for r in range(count):
            pre = pre + lax.dot_general(
                refs[r][...], refs[count + r][:features, :], (((0,), (0,)), ((), ())),
                preferred_element_type=F32,
            )
        pre = pre + b_ref[...]
        pre_ref[...] = pre
        hidden_ref[:rows, :] = jnp.maximum(pre, 0.0).astype(BF16)
        row = lax.broadcasted_iota(jnp.int32, (16, width), 0)
        lists = jnp.zeros((16, width), F32)
        for r in range(count):
            one = refs[count + r][features:, :].astype(F32)[:1]
            lists = jnp.where(row == r, one, lists)
        hidden_ref[rows:, :] = lists.astype(BF16)

    return pl.pallas_call(
        kernel,
        in_specs=[VMEM] * (2 * count + 1),
        out_specs=[VMEM] * 2,
        out_shape=[
            jax.ShapeDtypeStruct((rows, width), F32),
            jax.ShapeDtypeStruct((rows + 16, width), BF16),
        ],
        compiler_params=BIG,
        name="hidden_layer",
    )(*parts, *weights, bias)


def row_weights(tiles, dst_ids, blocks):
    total, side, _ = tiles.shape
    step = group_of(total, 32)
    unroll = group_of(step, 8)
    steps = total // step

    def kernel(dst_s, tile_ref, out_ref, acc):
        i = pl.program_id(0)

        @pl.when(i == 0)
        def _():
            acc[...] = jnp.zeros_like(acc)

        def body(g, carry):
            for u in range(unroll):
                t = g * unroll + u
                acc[dst_s[i * step + t]] += tile_ref[t].astype(F32)
            return carry

        lax.fori_loop(0, step // unroll, body, 0)

        @pl.when(i == steps - 1)
        def _():
            for b in range(blocks):
                out_ref[b] = jnp.broadcast_to(
                    jnp.sum(acc[b], axis=1, keepdims=True), (side, side)
                )

    return pl.pallas_call(
        kernel,
        grid_spec=pltpu.PrefetchScalarGridSpec(
            num_scalar_prefetch=1,
            grid=(steps,),
            in_specs=[pl.BlockSpec((step, side, side), lambda i, *_: (i, 0, 0))],
            out_specs=pl.BlockSpec((blocks, side, side), lambda i, *_: (0, 0, 0)),
            scratch_shapes=[pltpu.VMEM((blocks, side, side), F32)],
        ),
        out_shape=jax.ShapeDtypeStruct((blocks, side, side), F32),
        compiler_params=BIG,
        cost_estimate=pl.CostEstimate(
            flops=2 * total * side * side, bytes_accessed=2 * total * side * side, transcendentals=0
        ),
        name="row_weights",
    )(dst_ids, tiles)


def output_layer(
    tiles, dst_ids, src_ids, place, me, pools, weight, hidden, w_self, w_neigh, bias, labels,
    scale, n_feat,
):
    total, side, _ = tiles.shape
    blocks = weight.shape[0]
    width = hidden.shape[1]
    count = len(pools)
    per_pool = pools[0].shape[0]
    classes = w_self.shape[0]
    second = -(-classes // 8) * 8
    share = -(-(2 * second + 8) // (8 * n_feat)) * 8
    step = group_of(total, 96)
    unroll = group_of(step, 96)
    steps = total // step
    lead = (((0,), (0,)), ((), ()))
    last = (((1,), (1,)), ((), ()))

    def kernel(
        dst_s, src_s, place_s, me_s, tile_ref, weight_ref, hidden_ref, ws_ref, wn_ref, bias_ref,
        labels_ref, *refs,
    ):
        pool_refs = refs[:count]
        third_refs = refs[count : count + n_feat]
        gnum_ref, own_ref, acc, pool_ref, sums_ref, sems = refs[count + n_feat :]
        i = pl.program_id(0)

        @pl.when(i == 0)
        def _():
            copies = [
                pltpu.make_async_copy(
                    pool_refs[j], pool_ref.at[pl.ds(j * per_pool, per_pool)], sems.at[j]
                )
                for j in range(count)
            ]
            for copy in copies:
                copy.start()
            acc[...] = jnp.zeros_like(acc)
            for copy in copies:
                copy.wait()

        def body(g, carry):
            products = []
            for u in range(unroll):
                t = g * unroll + u
                products.append(
                    jnp.dot(
                        tile_ref[t],
                        pool_ref[place_s[src_s[i * step + t]]],
                        preferred_element_type=F32,
                    )
                )
            for u in range(unroll):
                acc[dst_s[i * step + g * unroll + u]] += products[u]
            return carry

        lax.fori_loop(0, step // unroll, body, 0)

        @pl.when(i == steps - 1)
        def _():
            gws = jnp.zeros((classes, width), F32)
            gwn = jnp.zeros((classes, width), F32)
            gb = jnp.zeros((1, classes), F32)
            for b in range(blocks):
                rows = slice(b * side, (b + 1) * side)
                under = weight_ref[b][:, :1]
                mean = (acc[b] / under).astype(BF16)
                own = hidden_ref[rows, :]
                logits = (
                    lax.dot_general(own, ws_ref[...], last, preferred_element_type=F32)
                    + lax.dot_general(mean, wn_ref[...], last, preferred_element_type=F32)
                    + bias_ref[...]
                )
                expo = jnp.exp(logits - jnp.max(logits, axis=1, keepdims=True))
                prob = expo / jnp.sum(expo, axis=1, keepdims=True)
                lane = lax.broadcasted_iota(jnp.int32, (side, classes), 1)
                onehot = jnp.where(labels_ref[rows, :] == lane, 1.0, 0.0)
                grad = (prob - onehot) * scale
                glog = grad.astype(BF16)
                gb = gb + jnp.sum(grad, axis=0, keepdims=True)
                gws = gws + lax.dot_general(glog, own, lead, preferred_element_type=F32)
                gwn = gwn + lax.dot_general(glog, mean, lead, preferred_element_type=F32)
                back = jnp.dot(glog, wn_ref[...], preferred_element_type=F32)
                gnum_ref[b] = (back / under).astype(BF16)
                own_ref[rows, :] = jnp.dot(glog, ws_ref[...], preferred_element_type=F32)
            sums_ref[...] = jnp.zeros_like(sums_ref)
            sums_ref[:classes, :] = gws
            sums_ref[second : second + classes, :] = gwn
            sums_ref[2 * second : 2 * second + 1, :classes] = gb
            for r in range(n_feat):
                start = pl.multiple_of((me_s[0] ^ r) * share, 8)
                third_refs[r][...] = sums_ref[pl.ds(start, share), :]

    def whole(*shape):
        return pl.BlockSpec(shape, lambda i, *_: (0,) * len(shape))

    rows = blocks * side
    out = [((share, width), F32)] * n_feat + [
        ((blocks, side, width), BF16),
        ((rows, width), F32),
    ]
    return pl.pallas_call(
        kernel,
        grid_spec=pltpu.PrefetchScalarGridSpec(
            num_scalar_prefetch=4,
            grid=(steps,),
            in_specs=[
                pl.BlockSpec((step, side, side), lambda i, *_: (i, 0, 0)),
                whole(blocks, side, side),
                whole(rows + 16, width),
                whole(classes, width),
                whole(classes, width),
                whole(1, classes),
                whole(rows, 1),
            ]
            + [pl.BlockSpec(memory_space=pl.ANY)] * count,
            out_specs=[whole(*s) for s, _ in out],
            scratch_shapes=[
                pltpu.VMEM((blocks, side, width), F32),
                pltpu.VMEM((count * per_pool, side, width), BF16),
                pltpu.VMEM((n_feat * share, width), F32),
                pltpu.SemaphoreType.DMA((count,)),
            ],
        ),
        out_shape=[jax.ShapeDtypeStruct(s, d) for s, d in out],
        compiler_params=BIG,
        cost_estimate=products_cost(total, side, width),
        name="output_layer",
    )(
        dst_ids, src_ids, place, me, tiles, weight, hidden, w_self, w_neigh,
        bias.reshape(1, classes), labels, *pools,
    )


def slot_gradients(tiles, dst_ids, src_ids, owners, mine, gnum, arrays):
    total, side, _ = tiles.shape
    blocks, _, width = gnum.shape
    slots = mine.shape[0]
    devices = owners.shape[0]
    each = slots // devices
    plane = devices // arrays
    step = group_of(total, 96)
    unroll = group_of(step, 96)
    steps = total // step

    def kernel(dst_s, src_s, owner_s, mine_s, tile_ref, gnum_ref, *refs):
        outs = refs[:arrays]
        acc, stage, sems = refs[arrays:]
        i = pl.program_id(0)

        @pl.when(i == 0)
        def _():
            acc[...] = jnp.zeros_like(acc)

        def body(g, carry):
            products = []
            for u in range(unroll):
                t = g * unroll + u
                products.append(
                    lax.dot_general(
                        tile_ref[t], gnum_ref[dst_s[i * step + t]],
                        (((0,), (0,)), ((), ())), preferred_element_type=F32,
                    )
                )
            for u in range(unroll):
                acc[src_s[i * step + g * unroll + u]] += products[u]
            return carry

        lax.fori_loop(0, step // unroll, body, 0)

        @pl.when(i == steps - 1)
        def _():
            copies = [
                pltpu.make_async_copy(stage.at[a % 2], outs[a], sems.at[a]) for a in range(arrays)
            ]
            for a in range(arrays):
                if a >= 2:
                    copies[a - 2].wait()

                def place(p, carry, a=a):
                    first = owner_s[a * plane + p] * each
                    for b in range(blocks):
                        stage[a % 2, p * blocks + b] = jnp.zeros((side, width), BF16)
                    for c in range(each):
                        target = p * blocks + mine_s[first + c]
                        stage[a % 2, target] = acc[first + c].astype(BF16)
                    return carry

                lax.fori_loop(0, plane, place, 0)
                copies[a].start()
            for a in range(max(arrays - 2, 0), arrays):
                copies[a].wait()

    shape = (plane * blocks, side, width)
    return pl.pallas_call(
        kernel,
        grid_spec=pltpu.PrefetchScalarGridSpec(
            num_scalar_prefetch=4,
            grid=(steps,),
            in_specs=[
                pl.BlockSpec((step, side, side), lambda i, *_: (i, 0, 0)),
                pl.BlockSpec(gnum.shape, lambda i, *_: (0, 0, 0)),
            ],
            out_specs=[pl.BlockSpec(memory_space=pl.ANY)] * arrays,
            scratch_shapes=[
                pltpu.VMEM((slots, side, width), F32),
                pltpu.VMEM((2,) + shape, BF16),
                pltpu.SemaphoreType.DMA((arrays,)),
            ],
        ),
        out_shape=[jax.ShapeDtypeStruct(shape, BF16)] * arrays,
        compiler_params=BIG,
        cost_estimate=products_cost(total, side, width),
        name="slot_gradients",
    )(dst_ids, src_ids, owners, mine, tiles, gnum)


def first_gradients(returned, own, pre, parts):
    terms = len(returned)
    rows, width = own.shape
    count = len(parts)
    features = parts[0].shape[0]

    def kernel(*refs):
        own_ref, pre_ref = refs[terms : terms + 2]
        part_refs = refs[terms + 2 : terms + 2 + count]
        outs = refs[terms + 2 + count :]
        grad = refs[0][...].astype(F32)
        for term in range(1, terms):
            grad = grad + refs[term][...].astype(F32)
        grad = grad + own_ref[...]
        grad_pre = jnp.where(pre_ref[...] > 0.0, grad, 0.0).astype(BF16)
        gb = jnp.sum(grad_pre.astype(F32), axis=0, keepdims=True)
        for r in range(count):
            outs[r][:features] = jnp.dot(part_refs[r][...], grad_pre, preferred_element_type=F32)
            outs[r][features:] = jnp.broadcast_to(gb, (8, width))

    shape = (features + 8, width)
    return pl.pallas_call(
        kernel,
        in_specs=[VMEM] * (terms + 2 + count),
        out_specs=[VMEM] * count,
        out_shape=[jax.ShapeDtypeStruct(shape, F32)] * count,
        compiler_params=BIG,
        name="first_gradients",
    )(*returned, own, pre, *parts)


def swap(value, axis, mask):
    return lax.ppermute(value, axis, [(k, k ^ mask) for k in range(lax.axis_size(axis))])


def feat_sum(pieces):
    total = pieces[0]
    for r in range(1, len(pieces)):
        total = total + swap(pieces[r], "feat", r)
    return total


def gather_blocks(value, planes, across, rows, beside):
    n_dom = lax.axis_size("dom")
    down = lax.axis_size("feat") // 2
    held, tails = [], []
    shifted = [value] + [swap(value, "dom", across * k) for k in range(1, planes)]
    for k, own in enumerate(shifted):
        if k > 0:
            own, beside = lax.optimization_barrier((own, beside))
        aside = [own] + [swap(own, "dom", i) for i in range(1, across)]
        below = [own] + [swap(own, "feat", 2 * j) for j in range(1, down)]
        pieces = list(aside)
        for j in range(1, down):
            pieces.append(below[j])
            for i in range(1, across):
                if k % 2 == 0:
                    pieces.append(swap(aside[i], "feat", 2 * j))
                else:
                    pieces.append(swap(below[j], "dom", i))
        held.append(jnp.concatenate([piece[:rows] for piece in pieces]))
        tails += [piece[rows:] for piece in aside]
    return held + [swap(piece, "feat", 1) for piece in held], jnp.stack(tails)


def total_of(values):
    total = values[0].astype(F32)
    for value in values[1:]:
        total = total + value.astype(F32)
    return total.astype(BF16)


def return_blocks(arrays, planes, across):
    down = lax.axis_size("feat") // 2
    size = arrays[0].shape[0] // (across * down)
    width = arrays[0].shape[-1]
    terms = []
    for k in list(range(1, planes)) + [0]:
        other = swap(arrays[planes + k], "feat", 1)
        pair = {}
        for j in reversed(range(down)):
            for i in reversed(range(across)):
                at = slice((j * across + i) * size, (j * across + i + 1) * size)
                pair[i, j] = total_of([arrays[k][at], other[at]]).reshape(-1, width)
        parts = [pair[0, 0]]
        for i in range(1, across):
            piece = [pair[i, 0]]
            if k % 2 == 0:
                piece += [swap(pair[i, j], "feat", 2 * j) for j in range(1, down)]
            parts.append(swap(total_of(piece), "dom", i))
        for j in range(1, down):
            piece = [pair[0, j]]
            if k % 2 == 1:
                piece += [swap(pair[i, j], "dom", i) for i in range(1, across)]
            parts.append(swap(total_of(piece), "feat", 2 * j))
        if k > 0:
            parts = [swap(total_of(parts), "dom", across * k)]
        terms += parts
    return terms


def doubling_sum(value, axis):
    size = lax.axis_size(axis)
    reach = 1
    while reach < size:
        value = value + swap(value, axis, reach)
        reach *= 2
    return value


def on_device(
    inputs_t, tiles_first, first_dst, first_src, w1_self, w1_neigh, bias_first, fetch_ids,
    tiles_out, out_dst, out_src, output_self_weight, output_neighbour_weight, bias_out, labels,
):
    n_feat = lax.axis_size("feat")
    devices = lax.axis_size("dom") * n_feat
    side = tiles_out.shape[1]
    rows_dev = labels.shape[0]
    blocks = rows_dev // side
    slots_peer = fetch_ids.shape[2]
    features, width = w1_self.shape
    classes = output_self_weight.shape[1]
    scale = 1.0 / math.sqrt(devices * rows_dev)

    me_dom, me_feat = lax.axis_index("dom"), lax.axis_index("feat")
    me = me_feat.astype(jnp.int32).reshape(1)
    planes = math.gcd(lax.axis_size("dom"), 4)
    across = lax.axis_size("dom") // planes

    listed = jnp.pad(
        fetch_ids.reshape(1, -1).astype(BF16), ((0, 15), (0, width - devices * slots_peer))
    )
    weights = jnp.concatenate([w1_neigh, w1_self, listed])
    weights = [weights] + [swap(weights, "feat", r) for r in range(1, n_feat)]
    parts = first_layer(inputs_t, tiles_first, first_dst, first_src, me, n_feat * blocks, n_feat)
    parts = [parts[0]] + [swap(parts[r], "feat", r) for r in range(1, n_feat)]
    pre, hidden = hidden_layer(parts, weights, bias_first.reshape(1, width))
    hidden, dst = lax.optimization_barrier((hidden, out_dst))
    weight = row_weights(tiles_out, dst, blocks)
    index = jnp.arange(devices, dtype=jnp.int32)
    plane = devices // (2 * planes)
    to_dom = me_dom ^ (index // plane % planes * across + index % across)
    to_feat = me_feat ^ (index % plane // across * 2 + index // (plane * planes))
    owners = (to_dom * n_feat + to_feat).astype(jnp.int32)
    here = me_dom * n_feat + me_feat
    pools, lists = gather_blocks(hidden, planes, across, rows_dev, weight)
    pools = [pool.reshape(-1, side, width) for pool in pools]
    mine = lax.dynamic_slice_in_dim(lists[:, :n_feat], here * slots_peer, slots_peer, axis=2)
    mine = mine.reshape(devices, slots_peer).astype(jnp.int32)
    mine = jnp.take(mine, index ^ here, axis=0)
    off = index[:, None] ^ here
    place = off % 2 * planes + off // n_feat // across
    place = (place * (n_feat // 2) + off % n_feat // 2) * across + off // n_feat % across
    place = (place * blocks + mine).reshape(-1)
    mine = mine.reshape(-1)
    column = labels.reshape(rows_dev, 1)
    *third, gnum, own = output_layer(
        tiles_out, out_dst, out_src, place, me, pools, weight, hidden, output_self_weight.T,
        output_neighbour_weight.T, bias_out, column, scale, n_feat,
    )
    third = [third[0]] + [swap(third[r], "feat", r) for r in range(1, n_feat)]
    arrays = slot_gradients(
        tiles_out, out_dst, out_src, owners, mine, gnum, 2 * planes
    )
    arrays, third = lax.optimization_barrier((arrays, third))
    third = doubling_sum(functools.reduce(jnp.add, third), "dom")
    third = jnp.stack([third] + [swap(third, "feat", r) for r in range(1, n_feat)])
    third = jnp.take(third, jnp.arange(n_feat) ^ me_feat, axis=0).reshape(-1, width)
    second = -(-classes // 8) * 8
    terms = return_blocks(arrays, planes, across)
    pieces = first_gradients(terms, own, pre, parts)
    last = doubling_sum(feat_sum(pieces), "dom")
    edge = 2 * features
    return (
        last[features:edge],
        last[:features],
        last[edge],
        third[:classes].T,
        third[second : second + classes].T,
        third[2 * second, :classes],
    )


def solution(mesh):
    in_specs = (
        P("feat", "dom"),
        P("dom", None, None),
        P("dom"),
        P("dom"),
        P("feat", None),
        P("feat", None),
        P(),
        P(None, ("dom", "feat"), None),
        P(("dom", "feat"), None, None),
        P(("dom", "feat")),
        P(("dom", "feat")),
        P(),
        P(),
        P(),
        P(("dom", "feat")),
    )
    out_specs = (P("feat", None), P("feat", None), P(), P(), P(), P())
    return jax.shard_map(
        on_device, mesh=mesh, in_specs=in_specs, out_specs=out_specs, check_vma=False
    )
```
